128 devices in a mesh: loop: 8 (over y, z_lo), mem: 16 (over x, z_hi, core).
Axes of the slice: x: 4, y: 4, z: 4 (z_hi: 2, z_lo: 2; z = z_hi * 2 + z_lo), core: 2. Of those that a mesh axis runs over, the one named last changes fastest.
Arguments:
- memory: bfloat16 [131072, 512], P('mem'), may hold values from -14 to 14
- sectioned_rows: bfloat16 [131072, 512], P(('loop', 'mem')), may hold values from -6 to 6
- sectioned_index: int32 [131072], P(('loop', 'mem')), may hold values from 0 to 8191, as said below
- src_local: int32 [131072], P(('loop', 'mem')), may hold values from 0 to 8191
- messages: bfloat16 [131072, 256], P(('loop', 'mem')), may hold values from -6 to 6
- block_owner: int32 [16384, 1], P(('loop', 'mem')), may hold values from 0 to 15; in each aligned block of 128 rows (0 to 127, 128 to 255, ...) at most 16 rows name the same one
- block_local: int32 [16384], P(('loop', 'mem')), may hold values from 0 to 255
- block_len: int32 [16384], P(('loop', 'mem')), may hold values from 1 to 32
- w_query: bfloat16 [768, 512], replicated, may hold values from -0.21875 to 0.21875
- w_key: bfloat16 [512, 512], replicated, may hold values from -0.25 to 0.25
- w_value: bfloat16 [512, 512], replicated, may hold values from -0.25 to 0.25
- w_input: bfloat16 [768, 1536], replicated, may hold values from -0.21875 to 0.21875
- w_hidden: bfloat16 [512, 1536], replicated, may hold values from -0.25 to 0.25
Outputs:
- new_rows: bfloat16 [131072, 512], P(('loop', 'mem'))
The draws below stay inside these ranges and needn't reach their ends.
Inputs may be any that keep to these rules, and one draw needn't show every extreme that they name: `block_owner`: within the 128 requests of one device no owner is named more than 16 times, a bound that some block reaches. `sectioned_index`: distinct within the 1024 rows of one device.
All inputs are finite; a program needn't handle non-finite values.
Results may differ from the reference program's by a relative error of at most 0.012.
The reference program's roundings to bfloat16 on the way count: a program that leaves them out, or rounds other values in their place, can miss the bound.
Values may be sent and summed in bfloat16 or wider, within the bound.
No kernel may reach another device: no remote copies, remote signals or barrier semaphores. Data moves between devices by JAX's collectives and lax.ppermute only.
A program may use at most 128 MiB of HBM per device.

```python
import math
import jax
import jax.numpy as jnp
import numpy as np
from jax import lax

DM = 512
MSG = 256
HEADS = 2
HEAD_DIM = 256
BR = 32
G = 8
NBLK = 128
NODES_DEV = 8192
E_DEV = 1024
CAP = 16
BLOCKS_DEV = 256
NODES = 131072
EVENTS = 131072
REQS = 16384
N_LOOP = 8
N_MEM = 16


def draw_memory(key, part):
    key = jax.random.fold_in(key, 11)
    values = jnp.clip(jax.random.normal(key, (NODES, DM), jnp.float32), -6.0, 6.0)
    return values.astype(jnp.bfloat16)


def draw_sectioned_index(key, part):
    key = jax.random.fold_in(key, 23)
    devices_count = EVENTS // E_DEV
    keys_all = jax.random.split(key, devices_count)
    chosen = jax.vmap(lambda single: jax.random.permutation(single, NODES_DEV)[:E_DEV])(keys_all)
    return chosen.reshape(-1).astype(jnp.int32)


def plant(values, key, least, largest):
    longest = values.shape.index(max(values.shape))
    spots = []
    for shift in (0, 1):
        where = [jax.random.randint(jax.random.fold_in(key, axis), (), 0, length) for axis, length in enumerate(values.shape)]
        where[longest] = (where[longest] + shift) % values.shape[longest]
        spots.append(tuple(where))
    return values.at[spots[0]].set(least).at[spots[1]].set(largest)


def steps_of(key, dims, shards, smallest, top_value):
    def one(position, parts):
        heights = jax.random.uniform(jax.random.fold_in(jax.random.fold_in(key, 6), position), (parts,), jnp.float32, smallest / len(shards), top_value / len(shards))
        return jnp.repeat(jnp.exp(heights), dims[position] // parts).reshape((-1,) + (1,) * (len(dims) - position - 1))

    level = one(*shards[0])
    for cut in shards[1:]:
        level = level * one(*cut)
    return level


def deal_out(key, own, number, rows, count, top, most, skew):
    order = jax.random.permutation(key, count)
    packed, ordinary = portions_of(count, rows * top, most, skew, True), portions_of(count, rows * top, most, skew, False)
    places = jnp.arange(count)

    def named(sizes, rotation):
        used = int((sizes > 0).sum())
        fixed = max(1, used // 4)
        passed = fixed + (places - fixed + rotation * (used - fixed)) % max(1, count - fixed)
        return jnp.zeros((count,), jnp.int32).at[order[jnp.where(places < fixed, places, passed)]].set(jnp.asarray(sizes, jnp.int32))

    sizes = jnp.where(number % 4 == 0, named(packed, number // 4), named(ordinary, number - number // 4 - 1))
    mixed = jax.random.permutation(jax.random.fold_in(own, 3), count)
    source_of, sink = mixed[0:count // 2 * 2:2], mixed[1:count // 2 * 2:2]
    slack = jnp.minimum(sizes[source_of] - 1, most - sizes[sink]) // 2
    slack = jnp.where((source_of == order[0]) | (sink == order[0]) | (sizes[sink] == 0), 0, jnp.maximum(slack, 0))
    passed = jax.random.randint(jax.random.fold_in(own, 4), (count // 2,), 0, 1 << 20) % (slack + 1)
    sizes = sizes.at[source_of].add(-passed).at[sink].add(passed)
    members = jnp.searchsorted(jnp.cumsum(sizes), jnp.arange(rows * top), side="right").astype(jnp.int32)
    table = members.reshape(top, rows).T
    table = table[jax.random.permutation(jax.random.fold_in(own, 1), rows)]
    rotation = jax.random.randint(jax.random.fold_in(own, 2), (rows, 1), 0, top)
    return jnp.take_along_axis(table, (jnp.arange(top)[None, :] + rotation) % top, axis=1)


def portions_of(amount, total, bound, lean, full):
    weights = [(1 << 20) // math.isqrt(standing ** lean) + 1 for standing in range(1, amount + 1)]
    largest = bound if full else min(bound, max(-(-total // amount), total * weights[0] // sum(weights)))
    least = 1 if total - largest >= amount - 1 else 0
    holding, rest = [largest] + [least] * (amount - 1), total - largest - least * (amount - 1)
    while rest > 0:
        free = [i for i in range(1, amount) if holding[i] < largest] or [i for i in range(1, amount) if holding[i] < bound]
        pool, budget = sum([weights[i] for i in free]), rest
        for i in free:
            more = min(bound - holding[i], max(1, budget * weights[i] // pool), rest)
            holding[i] = holding[i] + more
            rest = rest - more
    return np.array(holding)


def normal_values(key, extent, spread, most, cuts=(), kind=jnp.bfloat16):
    gain = steps_of(key, extent, cuts, -0.22, 0.18) if cuts else 1.0
    values = jax.random.normal(key, extent, jnp.float32) * spread * gain
    return jnp.minimum(jnp.maximum(values, -most), most).astype(kind)


def setup_inputs(seed: int = 0) -> dict:
    key_list = jax.random.split(jax.random.key(seed), 14)
    memory = draw_memory(jax.random.fold_in(key_list[13], 71), 0)
    sectioned_rows = normal_values(key_list[1], (EVENTS, DM), 1.0, 6.0, ((0, 128),))
    sectioned_index = draw_sectioned_index(jax.random.fold_in(key_list[13], 71), 0)
    src_local = plant(jax.random.randint(key_list[3], (EVENTS,), 0, NODES_DEV), jax.random.fold_in(key_list[3], 1), 0, NODES_DEV - 1).astype(jnp.int32)
    messages = normal_values(key_list[4], (EVENTS, MSG), 1.0, 6.0, ((0, 128),))
    block_owner_keys = jax.random.split(jax.random.fold_in(key_list[5], 1), REQS // NBLK)
    block_owner_turns = jax.random.permutation(jax.random.fold_in(key_list[5], 3), REQS // NBLK)
    block_owner = jax.vmap(lambda own, number: deal_out(jax.random.fold_in(key_list[5], 2), own, number, NBLK, N_MEM, 1, CAP, 2))(block_owner_keys, block_owner_turns).reshape((REQS, 1))
    block_local = plant(jax.random.randint(key_list[6], (REQS,), 0, BLOCKS_DEV), jax.random.fold_in(key_list[6], 1), 0, BLOCKS_DEV - 1).astype(jnp.int32)
    block_len = plant(jax.random.randint(key_list[7], (REQS,), 1, BR + 1), jax.random.fold_in(key_list[7], 1), 1, BR).astype(jnp.int32)
    w_query = normal_values(key_list[8], (DM + MSG, DM), (DM + MSG) ** -0.5, 0.21875)
    w_key = normal_values(key_list[9], (DM, DM), DM ** -0.5, 0.25)
    w_value = normal_values(key_list[10], (DM, DM), DM ** -0.5, 0.25)
    w_input = normal_values(key_list[11], (MSG + DM, 3 * DM), (MSG + DM) ** -0.5, 0.21875)
    w_hidden = normal_values(key_list[12], (DM, 3 * DM), DM ** -0.5, 0.25)
    return {"memory": memory, "sectioned_rows": sectioned_rows, "sectioned_index": sectioned_index, "src_local": src_local, "messages": messages, "block_owner": block_owner, "block_local": block_local, "block_len": block_len, "w_query": w_query, "w_key": w_key, "w_value": w_value, "w_input": w_input, "w_hidden": w_hidden}


def event_update(source_rows, message_rows, neighbours, lengths, w_query, w_key, w_value, w_input, w_hidden):
    count = neighbours.shape[0]
    flat = neighbours.reshape(count * BR, DM)
    key_rows = jnp.dot(flat, w_key, preferred_element_type=jnp.float32).astype(jnp.bfloat16).reshape(count, BR, HEADS, HEAD_DIM)
    value_rows = jnp.dot(flat, w_value, preferred_element_type=jnp.float32).astype(jnp.bfloat16).reshape(count, BR, HEADS, HEAD_DIM)
    joined = jnp.concatenate([source_rows, message_rows], 1)
    queries = jnp.dot(joined, w_query, preferred_element_type=jnp.float32).astype(jnp.bfloat16).reshape(count, G, HEADS, HEAD_DIM)
    scores = jnp.einsum('bghd,bkhd->bghk', queries.astype(jnp.float32), key_rows.astype(jnp.float32)) / math.sqrt(HEAD_DIM)
    usable = (jnp.arange(BR, dtype=jnp.int32)[None, :] < lengths[:, None])[:, None, None, :]
    scores = jnp.where(usable, scores, -jnp.inf)
    top_score = lax.optimization_barrier(jnp.max(scores, axis=-1, keepdims=True))
    expons = jnp.where(usable, jnp.exp(scores - top_score), 0.0)
    weights = (expons / lax.optimization_barrier(jnp.sum(expons, axis=-1, keepdims=True))).astype(jnp.bfloat16)
    attended = jnp.einsum('bghk,bkhd->bghd', weights.astype(jnp.float32), value_rows.astype(jnp.float32))
    attended = attended.reshape(count * G, DM).astype(jnp.bfloat16)
    input_gates = jnp.dot(jnp.concatenate([message_rows, attended], 1), w_input, preferred_element_type=jnp.float32)
    hidden_gates = jnp.dot(source_rows, w_hidden, preferred_element_type=jnp.float32)
    reset_gate = jax.nn.sigmoid(input_gates[:, :DM] + hidden_gates[:, :DM])
    update_gate = jax.nn.sigmoid(input_gates[:, DM:2 * DM] + hidden_gates[:, DM:2 * DM])
    candidate = jnp.tanh(input_gates[:, 2 * DM:] + reset_gate * hidden_gates[:, 2 * DM:])
    fresh = (1.0 - update_gate) * candidate + update_gate * source_rows.astype(jnp.float32)
    return fresh.astype(jnp.bfloat16)

def reference(memory, sectioned_rows, sectioned_index, src_local, messages, block_owner, block_local, block_len, w_query, w_key, w_value, w_input, w_hidden):
    group_events = N_MEM * E_DEV
    group_reqs = N_MEM * NBLK
    event_shard = jnp.arange(group_events, dtype=jnp.int32) // E_DEV * NODES_DEV
    results = []
    for group in range(N_LOOP):
        before = (group - 1) % N_LOOP
        pend_rows = sectioned_rows[before * group_events:(before + 1) * group_events]
        pend_index = sectioned_index[before * group_events:(before + 1) * group_events] + event_shard
        applied = memory.at[pend_index].set(pend_rows)
        first = group * group_events
        source_rows = applied[src_local[first:first + group_events] + event_shard]
        start_req = group * group_reqs
        owners = block_owner[start_req:start_req + group_reqs, 0]
        starts = owners * NODES_DEV + block_local[start_req:start_req + group_reqs] * BR
        neighbours = applied[starts[:, None] + jnp.arange(BR, dtype=jnp.int32)[None, :]]
        results.append(event_update(source_rows, messages[first:first + group_events], neighbours, block_len[start_req:start_req + group_reqs], w_query, w_key, w_value, w_input, w_hidden))
    return jnp.concatenate(results, 0)
```

```python
import jax
import jax.numpy as jnp
from jax import lax
from jax.experimental import pallas as pl
from jax.experimental.pallas import tpu as pltpu
from jax.sharding import PartitionSpec as P

DM = 512
HEADS = 2
HEAD_DIM = 256
BR = 32
G = 8
SPAN = 8
MASKED = -1e30


def shifted(block, axis, distance):
    size = lax.axis_size(axis)
    route = [((i - distance) % size, i) for i in range(size)]
    return lax.ppermute(block, axis, route)


def query_kernel(
    position, source_index, pending_index, pending, base, messages, w_query, slots, source, staged
):
    events = source_index.shape[0]
    chunk = 128
    staged[...] = jnp.zeros_like(staged)
    for start in range(0, events, chunk):
        rows = pl.ds(start, chunk)
        same = source_index[rows, :] == pending_index[...]
        picked = jnp.dot(
            jnp.where(same, 1.0, 0.0).astype(jnp.bfloat16),
            pending[...],
            preferred_element_type=jnp.float32,
        )
        hit = jnp.max(jnp.where(same, 1.0, 0.0), axis=1, keepdims=True) > 0.0
        merged = jnp.where(hit, picked, base[rows, :].astype(jnp.float32)).astype(jnp.bfloat16)
        source[rows, :] = merged
        found = jnp.dot(
            merged, w_query[:DM, :], preferred_element_type=jnp.float32
        ) + jnp.dot(messages[rows, :], w_query[DM:, :], preferred_element_type=jnp.float32)
        for item in range(chunk // G):
            place = pl.multiple_of(position[start // G + item] * G, G)
            staged[pl.ds(place, G), :] = found[item * G : (item + 1) * G, :]
    for start in range(0, slots.shape[0], 256):
        rows = pl.ds(start, 256)
        slots[rows, :] = staged[rows, :].astype(jnp.bfloat16)


def make_queries(position, source_index, pending_index, pending, base, messages, w_query, nslots):
    events = base.shape[0]
    vmem = pl.BlockSpec(memory_space=pltpu.VMEM)
    return pl.pallas_call(
        query_kernel,
        out_shape=(
            jax.ShapeDtypeStruct((nslots * G, DM), jnp.bfloat16),
            jax.ShapeDtypeStruct((events, DM), jnp.bfloat16),
        ),
        in_specs=[pl.BlockSpec(memory_space=pltpu.SMEM)] + [vmem] * 6,
        out_specs=(vmem, vmem),
        scratch_shapes=[pltpu.VMEM((nslots * G, DM), jnp.float32)],
        compiler_params=pltpu.CompilerParams(vmem_limit_bytes=40 * 1024 * 1024),
        cost_estimate=pl.CostEstimate(
            flops=4_000_000_000, bytes_accessed=8_000_000, transcendentals=0
        ),
        name="queries",
    )(position, source_index, pending_index, pending, base, messages, w_query)


STEP_SLOTS = 16


def attend_kernel(blocks, queries, lengths, pairs, attended, held, sems):
    step = pl.program_id(0)
    steps = pl.num_programs(0)

    def fetch(which, slot):
        for item in range(STEP_SLOTS):
            first = pl.multiple_of(blocks[which * STEP_SLOTS + item] * BR, BR)
            pltpu.make_async_copy(
                pairs.at[pl.ds(first, BR), :],
                held.at[slot, pl.ds(item * BR, BR), :],
                sems.at[slot],
            ).start()

    slot = lax.rem(step, 2)

    @pl.when(step == 0)
    def _():
        fetch(0, 0)

    @pl.when(step + 1 < steps)
    def _():
        fetch(step + 1, 1 - slot)

    pltpu.make_async_copy(
        pairs.at[pl.ds(0, STEP_SLOTS * BR), :], held.at[slot], sems.at[slot]
    ).wait()

    keys_wide = SPAN * BR
    rows_high = SPAN * G
    lane = lax.broadcasted_iota(jnp.int32, (rows_high, keys_wide), 1)
    row = lax.broadcasted_iota(jnp.int32, (rows_high, keys_wide), 0)
    own = (lane // BR) == (row // G)
    offset = lax.rem(lax.broadcasted_iota(jnp.int32, (1, keys_wide), 1), BR)
    groups = STEP_SLOTS // SPAN
    for group in range(groups):
        length = lengths[pl.ds(step * groups + group, 1), :]
        usable = own & (offset < length)
        for head in range(HEADS):
            query = queries[group * rows_high : (group + 1) * rows_high, head * HEAD_DIM : (head + 1) * HEAD_DIM]
            key = held[slot, group * keys_wide : (group + 1) * keys_wide, head * HEAD_DIM : (head + 1) * HEAD_DIM]
            value = held[
                slot,
                group * keys_wide : (group + 1) * keys_wide,
                DM + head * HEAD_DIM : DM + (head + 1) * HEAD_DIM,
            ]
            scores = lax.dot_general(
                query, key, (((1,), (1,)), ((), ())), preferred_element_type=jnp.float32
            ) * (1.0 / 16.0)
            scores = jnp.where(usable, scores, MASKED)
            top = jnp.max(scores, axis=1, keepdims=True)
            expons = jnp.where(usable, jnp.exp(scores - top), 0.0)
            total = jnp.maximum(jnp.sum(expons, axis=1, keepdims=True), 1e-30)
            weights = (expons / total).astype(jnp.bfloat16)
            result = jnp.dot(weights, value, preferred_element_type=jnp.float32)
            attended[
                group * rows_high : (group + 1) * rows_high, head * HEAD_DIM : (head + 1) * HEAD_DIM
            ] = result.astype(jnp.bfloat16)


def attend(blocks, queries, lengths, pairs):
    nslots = blocks.shape[0]
    steps = nslots // STEP_SLOTS
    return pl.pallas_call(
        attend_kernel,
        out_shape=jax.ShapeDtypeStruct(queries.shape, jnp.bfloat16),
        grid_spec=pltpu.PrefetchScalarGridSpec(
            num_scalar_prefetch=1,
            grid=(steps,),
            in_specs=[
                pl.BlockSpec((STEP_SLOTS * G, DM), lambda i, b: (i, 0)),
                pl.BlockSpec(lengths.shape, lambda i, b: (0, 0)),
                pl.BlockSpec(memory_space=pl.ANY),
            ],
            out_specs=pl.BlockSpec((STEP_SLOTS * G, DM), lambda i, b: (i, 0)),
            scratch_shapes=[
                pltpu.VMEM((2, STEP_SLOTS * BR, 2 * DM), jnp.bfloat16),
                pltpu.SemaphoreType.DMA((2,)),
            ],
        ),
        compiler_params=pltpu.CompilerParams(
            dimension_semantics=("arbitrary",), vmem_limit_bytes=32 * 1024 * 1024
        ),
        cost_estimate=pl.CostEstimate(
            flops=4_000_000_000, bytes_accessed=20_000_000, transcendentals=1_000_000
        ),
        name="attend",
    )(blocks, queries, lengths, pairs)


CHUNK = 128


def update_kernel(position, returned, both, fed, kept, source, w_input, fresh, wide, ordered):
    step = pl.program_id(0)

    @pl.when(step == 0)
    def _():
        for start in range(0, returned.shape[0], 256):
            rows = pl.ds(start, 256)
            wide[rows, :] = returned[rows, :].astype(jnp.float32)

    for item in range(CHUNK // G):
        place = pl.multiple_of(position[step * (CHUNK // G) + item] * G, G)
        ordered[pl.ds(item * G, G), :] = wide[pl.ds(place, G), :]
    attended = ordered[...].astype(jnp.bfloat16)
    gates = jnp.dot(attended, w_input[...], preferred_element_type=jnp.float32)
    reset = jax.nn.sigmoid(gates[:, :DM] + both[:, :DM])
    update = jax.nn.sigmoid(gates[:, DM : 2 * DM] + both[:, DM:])
    candidate = jnp.tanh(gates[:, 2 * DM :] + fed[...] + reset * kept[...])
    fresh[...] = (
        (1.0 - update) * candidate + update * source[...].astype(jnp.float32)
    ).astype(jnp.bfloat16)


def updated(position, returned, both, fed, kept, source, w_attended):
    events = source.shape[0]
    return pl.pallas_call(
        update_kernel,
        out_shape=jax.ShapeDtypeStruct((events, DM), jnp.bfloat16),
        grid_spec=pltpu.PrefetchScalarGridSpec(
            num_scalar_prefetch=1,
            grid=(events // CHUNK,),
            in_specs=[
                pl.BlockSpec(returned.shape, lambda i, p: (0, 0)),
                pl.BlockSpec((CHUNK, 2 * DM), lambda i, p: (i, 0)),
                pl.BlockSpec((CHUNK, DM), lambda i, p: (i, 0)),
                pl.BlockSpec((CHUNK, DM), lambda i, p: (i, 0)),
                pl.BlockSpec((CHUNK, DM), lambda i, p: (i, 0)),
                pl.BlockSpec(w_attended.shape, lambda i, p: (0, 0)),
            ],
            out_specs=pl.BlockSpec((CHUNK, DM), lambda i, p: (i, 0)),
            scratch_shapes=[
                pltpu.VMEM(returned.shape, jnp.float32),
                pltpu.VMEM((CHUNK, DM), jnp.float32),
            ],
        ),
        compiler_params=pltpu.CompilerParams(
            dimension_semantics=("arbitrary",), vmem_limit_bytes=40 * 1024 * 1024
        ),
        cost_estimate=pl.CostEstimate(
            flops=1_700_000_000, bytes_accessed=15_000_000, transcendentals=1_500_000
        ),
        name="update",
    )(position, returned, both, fed, kept, source, w_attended)


def body(
    memory,
    sectioned_rows,
    sectioned_index,
    src_local,
    messages,
    block_owner,
    block_local,
    block_len,
    w_query,
    w_key,
    w_value,
    w_input,
    w_hidden,
):
    shards = lax.axis_size("mem")
    me = lax.axis_index("mem")
    nblocks = block_local.shape[0]
    capacity = max(2, 2 * nblocks // shards)
    nslots = shards * capacity
    msg = messages.shape[1]

    pending_index = shifted(sectioned_index, "loop", 1)
    pending = shifted(sectioned_rows, "loop", 1)

    owners = block_owner[:, 0]
    onehot = (owners[:, None] == jnp.arange(shards, dtype=jnp.int32)[None, :]).astype(jnp.int32)
    rank = jnp.sum((jnp.cumsum(onehot, 0) - onehot) * onehot, 1)
    position = owners * capacity + rank
    wanted = jnp.zeros((nslots,), jnp.int32).at[position].set(block_local * 64 + block_len)
    asked = lax.all_gather(wanted.reshape(shards, capacity), "mem")
    asked = lax.dynamic_index_in_dim(asked, me, 1, keepdims=False).reshape(nslots)
    blocks = asked // 64
    lengths = jnp.repeat(asked % 64, BR).reshape(nslots // SPAN, SPAN * BR)

    base = memory[src_local]
    queries, source = make_queries(
        position, src_local[:, None], pending_index[None, :], pending, base, messages, w_query, nslots
    )
    arrived = lax.all_to_all(
        queries.reshape(shards, capacity * G, DM), "mem", split_axis=0, concat_axis=0, tiled=True
    ).reshape(nslots * G, DM)

    applied = memory.at[pending_index].set(pending)
    pairs = jnp.dot(
        applied, jnp.concatenate([w_key, w_value], 1), preferred_element_type=jnp.float32
    ).astype(jnp.bfloat16)

    attended = attend(blocks, arrived, lengths, pairs)
    returned = lax.all_to_all(
        attended.reshape(shards, capacity * G, DM), "mem", split_axis=0, concat_axis=0, tiled=True
    ).reshape(nslots * G, DM)

    fed = jnp.dot(messages, w_input[:msg], preferred_element_type=jnp.float32)
    kept = jnp.dot(source, w_hidden, preferred_element_type=jnp.float32)
    both = fed[:, : 2 * DM] + kept[:, : 2 * DM]
    return updated(
        position, returned, both, fed[:, 2 * DM :], kept[:, 2 * DM :], source, w_input[msg:]
    )


def solution(mesh):
    placed = (
        P("mem", None),
        P(("loop", "mem"), None),
        P(("loop", "mem")),
        P(("loop", "mem")),
        P(("loop", "mem"), None),
        P(("loop", "mem"), None),
        P(("loop", "mem")),
        P(("loop", "mem")),
        P(),
        P(),
        P(),
        P(),
        P(),
    )
    return jax.shard_map(
        body, mesh=mesh, in_specs=placed, out_specs=P(("loop", "mem"), None), check_vma=False
    )
```

```python
import jax
import jax.numpy as jnp
from jax import lax
from jax.experimental import pallas as pl
from jax.experimental.pallas import tpu as pltpu
from jax.sharding import PartitionSpec as P

DM = 512
HEADS = 2
HEAD_DIM = 256
BR = 32
G = 8
VMEM = 60 * 1024 * 1024
SPAN = 8
MASKED = -1e30


def shifted(block, axis, distance):
    size = lax.axis_size(axis)
    route = [((i - distance) % size, i) for i in range(size)]
    return lax.ppermute(block, axis, route)


CHUNK = 128
TILE = 512
META = 16


def query_kernel(
    position, source_index, pending_index, pending, base, messages, w_query, notes, slots, source, staged
):
    step = pl.program_id(0)

    @pl.when(step == 0)
    def _():
        staged[...] = jnp.zeros_like(staged)

    same = source_index[...] == pending_index[...]
    chosen = jnp.where(same, 1.0, 0.0)
    hit = jnp.max(chosen, axis=1, keepdims=True) > 0.0
    picked = jnp.dot(chosen.astype(jnp.bfloat16), pending[...], preferred_element_type=jnp.float32)
    merged = jnp.where(hit, picked, base[...].astype(jnp.float32)).astype(jnp.bfloat16)
    source[...] = merged
    found = jnp.dot(merged, w_query[:DM, :], preferred_element_type=jnp.float32) + jnp.dot(
        messages[...], w_query[DM:, :], preferred_element_type=jnp.float32
    )
    for item in range(CHUNK // G):
        place = pl.multiple_of(position[step * (CHUNK // G) + item] * G, G)
        staged[pl.ds(place, G), :] = found[item * G : (item + 1) * G, :]

    @pl.when(step == pl.num_programs(0) - 1)
    def _():
        high = staged.shape[0] * META // notes.shape[0]
        for owner in range(notes.shape[0] // META):
            first = owner * (high + META)
            slots[first : first + high, :] = staged[owner * high : (owner + 1) * high, :].astype(
                jnp.bfloat16
            )
            slots[first + high : first + high + META, :] = notes[owner * META : (owner + 1) * META, :]


def make_queries(position, source_index, pending_index, pending, base, messages, w_query, notes, nslots):
    events, msg = messages.shape
    total = nslots * G + notes.shape[0]
    whole = lambda array: pl.BlockSpec(array.shape, lambda i, p: (0, 0))
    return pl.pallas_call(
        query_kernel,
        out_shape=(
            jax.ShapeDtypeStruct((total, DM), jnp.bfloat16),
            jax.ShapeDtypeStruct((events, DM), jnp.bfloat16),
        ),
        grid_spec=pltpu.PrefetchScalarGridSpec(
            num_scalar_prefetch=1,
            grid=(events // CHUNK,),
            in_specs=[
                pl.BlockSpec((CHUNK, 1), lambda i, p: (i, 0)),
                whole(pending_index),
                whole(pending),
                pl.BlockSpec((CHUNK, DM), lambda i, p: (i, 0)),
                pl.BlockSpec((CHUNK, msg), lambda i, p: (i, 0)),
                whole(w_query),
                whole(notes),
            ],
            out_specs=(
                pl.BlockSpec((total, DM), lambda i, p: (0, 0)),
                pl.BlockSpec((CHUNK, DM), lambda i, p: (i, 0)),
            ),
            scratch_shapes=[pltpu.VMEM((nslots * G, DM), jnp.float32)],
        ),
        compiler_params=pltpu.CompilerParams(
            dimension_semantics=("arbitrary",), vmem_limit_bytes=VMEM
        ),
        cost_estimate=pl.CostEstimate(
            flops=2_000_000_000, bytes_accessed=8_000_000, transcendentals=0
        ),
        name="queries",
    )(position, source_index, pending_index, pending, base, messages, w_query, notes)


def pairs_kernel(pending_index, pending, memory, w_key, w_value, pairs):
    first = pl.program_id(0) * TILE
    row = first + lax.broadcasted_iota(jnp.int32, (TILE, 1), 0)
    chosen = jnp.where(row == pending_index[...], 1.0, 0.0)
    hit = jnp.max(chosen, axis=1, keepdims=True) > 0.0
    picked = jnp.dot(chosen.astype(jnp.bfloat16), pending[...], preferred_element_type=jnp.float32)
    merged = jnp.where(hit, picked, memory[...].astype(jnp.float32)).astype(jnp.bfloat16)
    pairs[:, :DM] = jnp.dot(merged, w_key[...], preferred_element_type=jnp.float32).astype(jnp.bfloat16)
    pairs[:, DM:] = jnp.dot(merged, w_value[...], preferred_element_type=jnp.float32).astype(jnp.bfloat16)


def make_pairs(pending_index, pending, memory, w_key, w_value):
    rows = memory.shape[0]
    whole = lambda array: pl.BlockSpec(array.shape, lambda i: (0, 0))
    return pl.pallas_call(
        pairs_kernel,
        out_shape=jax.ShapeDtypeStruct((rows, 2 * DM), jnp.bfloat16),
        grid=(rows // TILE,),
        in_specs=[
            whole(pending_index),
            whole(pending),
            pl.BlockSpec((TILE, DM), lambda i: (i, 0)),
            whole(w_key),
            whole(w_value),
        ],
        out_specs=pl.BlockSpec((TILE, 2 * DM), lambda i: (i, 0)),
        compiler_params=pltpu.CompilerParams(
            dimension_semantics=("arbitrary",), vmem_limit_bytes=VMEM
        ),
        cost_estimate=pl.CostEstimate(
            flops=17_200_000_000, bytes_accessed=28_000_000, transcendentals=0
        ),
        name="pairs",
    )(pending_index, pending, memory, w_key, w_value)


SEGMENTS = 4


def attend_kernel(blocks, queries, pairs, attended, held, sems):
    step = pl.program_id(0)
    steps = pl.num_programs(0)
    step_slots = held.shape[1] // BR
    capacity = step_slots // SEGMENTS
    segment = capacity * G + META

    def fetch(which, slot):
        for item in range(step_slots):
            first = pl.multiple_of(blocks[which * step_slots + item] * BR, BR)
            pltpu.make_async_copy(
                pairs.at[pl.ds(first, BR), :],
                held.at[slot, pl.ds(item * BR, BR), :],
                sems.at[slot],
            ).start()

    slot = lax.rem(step, 2)

    @pl.when(step == 0)
    def _():
        fetch(0, 0)

    @pl.when(step + 1 < steps)
    def _():
        fetch(step + 1, 1 - slot)

    pltpu.make_async_copy(
        pairs.at[pl.ds(0, step_slots * BR), :], held.at[slot], sems.at[slot]
    ).wait()

    keys_wide = SPAN * BR
    rows_high = SPAN * G
    lane = lax.broadcasted_iota(jnp.int32, (rows_high, keys_wide), 1)
    row = lax.broadcasted_iota(jnp.int32, (rows_high, keys_wide), 0)
    own = (lane // BR) == (row // G)
    offset = lax.rem(lax.broadcasted_iota(jnp.int32, (1, keys_wide), 1), BR).astype(jnp.float32)
    groups = capacity // SPAN
    units = [
        (part, group, head)
        for part in range(SEGMENTS)
        for group in range(groups)
        for head in range(HEADS)
    ]
    scores = []
    for part, group, head in units:
        notes = queries[part * segment + capacity * G : (part + 1) * segment, :].astype(jnp.float32)
        length = notes[0:1, group * keys_wide : (group + 1) * keys_wide]
        usable = own & (offset < length)
        top = part * segment + group * rows_high
        query = queries[top : top + rows_high, head * HEAD_DIM : (head + 1) * HEAD_DIM]
        first = (part * groups + group) * keys_wide
        key = held[slot, first : first + keys_wide, head * HEAD_DIM : (head + 1) * HEAD_DIM]
        score = lax.dot_general(
            query, key, (((1,), (1,)), ((), ())), preferred_element_type=jnp.float32
        ) * (1.0 / 16.0)
        scores.append(jnp.where(usable, score, MASKED))
    scores = jnp.concatenate(scores, 0)
    expons = jnp.exp(scores - jnp.max(scores, axis=1, keepdims=True))
    weights = (expons * (1.0 / jnp.sum(expons, axis=1, keepdims=True))).astype(jnp.bfloat16)
    for number, (part, group, head) in enumerate(units):
        first = (part * groups + group) * keys_wide
        value = held[
            slot, first : first + keys_wide, DM + head * HEAD_DIM : DM + (head + 1) * HEAD_DIM
        ]
        result = jnp.dot(
            weights[number * rows_high : (number + 1) * rows_high],
            value,
            preferred_element_type=jnp.float32,
        )
        top = (part * groups + group) * rows_high
        attended[top : top + rows_high, head * HEAD_DIM : (head + 1) * HEAD_DIM] = result.astype(
            jnp.bfloat16
        )


def attend(blocks, queries, pairs, shards):
    nslots = blocks.shape[0]
    steps = shards // SEGMENTS
    return pl.pallas_call(
        attend_kernel,
        out_shape=jax.ShapeDtypeStruct((nslots * G, DM), jnp.bfloat16),
        grid_spec=pltpu.PrefetchScalarGridSpec(
            num_scalar_prefetch=1,
            grid=(steps,),
            in_specs=[
                pl.BlockSpec((queries.shape[0] // steps, DM), lambda i, b: (i, 0)),
                pl.BlockSpec(memory_space=pl.ANY),
            ],
            out_specs=pl.BlockSpec((nslots * G // steps, DM), lambda i, b: (i, 0)),
            scratch_shapes=[
                pltpu.VMEM((2, nslots // steps * BR, 2 * DM), jnp.bfloat16),
                pltpu.SemaphoreType.DMA((2,)),
            ],
        ),
        compiler_params=pltpu.CompilerParams(
            dimension_semantics=("arbitrary",), vmem_limit_bytes=VMEM
        ),
        cost_estimate=pl.CostEstimate(
            flops=4_000_000_000, bytes_accessed=20_000_000, transcendentals=1_000_000
        ),
        name="attend",
    )(blocks, queries, pairs)


def update_kernel(position, returned, both, fed, kept, source, w_input, fresh, wide, ordered):
    step = pl.program_id(0)

    @pl.when(step == 0)
    def _():
        for start in range(0, returned.shape[0], 256):
            rows = pl.ds(start, 256)
            wide[rows, :] = returned[rows, :].astype(jnp.float32)

    for item in range(CHUNK // G):
        place = pl.multiple_of(position[step * (CHUNK // G) + item] * G, G)
        ordered[pl.ds(item * G, G), :] = wide[pl.ds(place, G), :]
    attended = ordered[...].astype(jnp.bfloat16)
    gates = jnp.dot(attended, w_input[...], preferred_element_type=jnp.float32)
    reset = jax.nn.sigmoid(gates[:, :DM] + both[:, :DM])
    update = jax.nn.sigmoid(gates[:, DM : 2 * DM] + both[:, DM:])
    candidate = jnp.tanh(gates[:, 2 * DM :] + fed[...] + reset * kept[...])
    fresh[...] = (
        (1.0 - update) * candidate + update * source[...].astype(jnp.float32)
    ).astype(jnp.bfloat16)


def updated(position, returned, both, fed, kept, source, w_attended):
    events = source.shape[0]
    return pl.pallas_call(
        update_kernel,
        out_shape=jax.ShapeDtypeStruct((events, DM), jnp.bfloat16),
        grid_spec=pltpu.PrefetchScalarGridSpec(
            num_scalar_prefetch=1,
            grid=(events // CHUNK,),
            in_specs=[
                pl.BlockSpec(returned.shape, lambda i, p: (0, 0)),
                pl.BlockSpec((CHUNK, 2 * DM), lambda i, p: (i, 0)),
                pl.BlockSpec((CHUNK, DM), lambda i, p: (i, 0)),
                pl.BlockSpec((CHUNK, DM), lambda i, p: (i, 0)),
                pl.BlockSpec((CHUNK, DM), lambda i, p: (i, 0)),
                pl.BlockSpec(w_attended.shape, lambda i, p: (0, 0)),
            ],
            out_specs=pl.BlockSpec((CHUNK, DM), lambda i, p: (i, 0)),
            scratch_shapes=[
                pltpu.VMEM(returned.shape, jnp.float32),
                pltpu.VMEM((CHUNK, DM), jnp.float32),
            ],
        ),
        compiler_params=pltpu.CompilerParams(
            dimension_semantics=("arbitrary",), vmem_limit_bytes=VMEM
        ),
        cost_estimate=pl.CostEstimate(
            flops=1_700_000_000, bytes_accessed=15_000_000, transcendentals=1_500_000
        ),
        name="update",
    )(position, returned, both, fed, kept, source, w_attended)


def body(
    memory,
    sectioned_rows,
    sectioned_index,
    src_local,
    messages,
    block_owner,
    block_local,
    block_len,
    w_query,
    w_key,
    w_value,
    w_input,
    w_hidden,
):
    shards = lax.axis_size("mem")
    nblocks = block_local.shape[0]
    capacity = max(2, 2 * nblocks // shards)
    nslots = shards * capacity
    msg = messages.shape[1]

    pending_index = shifted(sectioned_index, "loop", 1)[None, :]
    pending = shifted(sectioned_rows, "loop", 1)

    owners = block_owner[:, 0]
    onehot = (owners[:, None] == jnp.arange(shards, dtype=jnp.int32)[None, :]).astype(jnp.int32)
    rank = jnp.sum((jnp.cumsum(onehot, 0) - onehot) * onehot, 1)
    position = owners * capacity + rank
    wanted = jnp.zeros((nslots,), jnp.int32).at[position].set(block_local * 64 + block_len)
    wanted = wanted.reshape(shards, capacity)
    notes = jnp.zeros((shards, META, DM), jnp.int32)
    notes = notes.at[:, 0, : capacity * BR].set(jnp.repeat(wanted % 64, BR, axis=1))
    notes = notes.at[:, 1, :capacity].set(wanted // 64)
    notes = notes.astype(jnp.bfloat16).reshape(shards * META, DM)

    base = memory[src_local]
    queries, source = make_queries(
        position, src_local[:, None], pending_index, pending, base, messages, w_query, notes, nslots
    )
    segment = capacity * G + META
    arrived = lax.all_to_all(
        queries.reshape(shards, segment, DM), "mem", split_axis=0, concat_axis=0, tiled=True
    )
    pairs = make_pairs(pending_index, pending, memory, w_key, w_value)
    blocks = arrived[:, capacity * G + 1, :capacity].astype(jnp.int32).reshape(nslots)
    attended = attend(blocks, arrived.reshape(shards * segment, DM), pairs, shards)
    returned = lax.all_to_all(
        attended.reshape(shards, capacity * G, DM), "mem", split_axis=0, concat_axis=0, tiled=True
    ).reshape(nslots * G, DM)

    fed = jnp.dot(messages, w_input[:msg], preferred_element_type=jnp.float32)
    kept = jnp.dot(source, w_hidden, preferred_element_type=jnp.float32)
    both = fed[:, : 2 * DM] + kept[:, : 2 * DM]
    return updated(
        position, returned, both, fed[:, 2 * DM :], kept[:, 2 * DM :], source, w_input[msg:]
    )


def solution(mesh):
    placed = (
        P("mem", None),
        P(("loop", "mem"), None),
        P(("loop", "mem")),
        P(("loop", "mem")),
        P(("loop", "mem"), None),
        P(("loop", "mem"), None),
        P(("loop", "mem")),
        P(("loop", "mem")),
        P(),
        P(),
        P(),
        P(),
        P(),
    )
    return jax.shard_map(
        body, mesh=mesh, in_specs=placed, out_specs=P(("loop", "mem"), None), check_vma=False
    )
```

```python
import jax
import jax.numpy as jnp
from jax import lax
from jax.experimental import pallas as pl
from jax.experimental.pallas import tpu as pltpu
from jax.sharding import PartitionSpec as P

DM = 512
HEADS = 2
HEAD_DIM = 256
BR = 32
G = 8
VMEM = 60 * 1024 * 1024
SPAN = 8
MASKED = -1e30


def shifted(block, axis, distance):
    size = lax.axis_size(axis)
    route = [((i - distance) % size, i) for i in range(size)]
    return lax.ppermute(block, axis, route)


CHUNK = 512
PART = 256
TILE = 512
META = 16


def query_kernel(
    position, source_index, pending_index, pending, base, messages, w_query, notes, slots, source, staged
):
    step = pl.program_id(0)

    @pl.when(step == 0)
    def _():
        staged[...] = jnp.zeros_like(staged)

    for start in range(0, CHUNK, 128):
        rows = slice(start, start + 128)
        same = source_index[rows, :] == pending_index[...]
        chosen = jnp.where(same, 1.0, 0.0)
        hit = jnp.max(chosen, axis=1, keepdims=True) > 0.0
        picked = jnp.dot(
            chosen.astype(jnp.bfloat16), pending[...], preferred_element_type=jnp.float32
        )
        merged = jnp.where(hit, picked, base[rows, :].astype(jnp.float32)).astype(jnp.bfloat16)
        source[rows, :] = merged
        found = jnp.dot(merged, w_query[:DM, :], preferred_element_type=jnp.float32) + jnp.dot(
            messages[rows, :], w_query[DM:, :], preferred_element_type=jnp.float32
        )
        for item in range(128 // G):
            place = pl.multiple_of(position[(step * CHUNK + start) // G + item] * G, G)
            staged[pl.ds(place, G), :] = found[item * G : (item + 1) * G, :]

    @pl.when(step == pl.num_programs(0) - 1)
    def _():
        high = staged.shape[0] * META // notes.shape[0]
        for owner in range(notes.shape[0] // META):
            first = owner * (high + META)
            slots[first : first + high, :] = staged[owner * high : (owner + 1) * high, :].astype(
                jnp.bfloat16
            )
            slots[first + high : first + high + META, :] = notes[owner * META : (owner + 1) * META, :]


def make_queries(position, source_index, pending_index, pending, base, messages, w_query, notes, nslots):
    events, msg = messages.shape
    total = nslots * G + notes.shape[0]
    whole = lambda array: pl.BlockSpec(array.shape, lambda i, p: (0, 0))
    return pl.pallas_call(
        query_kernel,
        out_shape=(
            jax.ShapeDtypeStruct((total, DM), jnp.bfloat16),
            jax.ShapeDtypeStruct((events, DM), jnp.bfloat16),
        ),
        grid_spec=pltpu.PrefetchScalarGridSpec(
            num_scalar_prefetch=1,
            grid=(events // CHUNK,),
            in_specs=[
                pl.BlockSpec((CHUNK, 1), lambda i, p: (i, 0)),
                whole(pending_index),
                whole(pending),
                pl.BlockSpec((CHUNK, DM), lambda i, p: (i, 0)),
                pl.BlockSpec((CHUNK, msg), lambda i, p: (i, 0)),
                whole(w_query),
                whole(notes),
            ],
            out_specs=(
                pl.BlockSpec((total, DM), lambda i, p: (0, 0)),
                pl.BlockSpec((CHUNK, DM), lambda i, p: (i, 0)),
            ),
            scratch_shapes=[pltpu.VMEM((nslots * G, DM), jnp.float32)],
        ),
        compiler_params=pltpu.CompilerParams(
            dimension_semantics=("arbitrary",), vmem_limit_bytes=VMEM
        ),
        cost_estimate=pl.CostEstimate(
            flops=2_000_000_000, bytes_accessed=8_000_000, transcendentals=0
        ),
        name="queries",
    )(position, source_index, pending_index, pending, base, messages, w_query, notes)


def pairs_kernel(pending_index, pending, memory, w_key, w_value, pairs):
    first = pl.program_id(0) * TILE
    row = first + lax.broadcasted_iota(jnp.int32, (TILE, 1), 0)
    chosen = jnp.where(row == pending_index[...], 1.0, 0.0)
    hit = jnp.max(chosen, axis=1, keepdims=True) > 0.0
    picked = jnp.dot(chosen.astype(jnp.bfloat16), pending[...], preferred_element_type=jnp.float32)
    merged = jnp.where(hit, picked, memory[...].astype(jnp.float32)).astype(jnp.bfloat16)
    pairs[:, :DM] = jnp.dot(merged, w_key[...], preferred_element_type=jnp.float32).astype(jnp.bfloat16)
    pairs[:, DM:] = jnp.dot(merged, w_value[...], preferred_element_type=jnp.float32).astype(jnp.bfloat16)


def make_pairs(pending_index, pending, memory, w_key, w_value):
    rows = memory.shape[0]
    whole = lambda array: pl.BlockSpec(array.shape, lambda i: (0, 0))
    return pl.pallas_call(
        pairs_kernel,
        out_shape=jax.ShapeDtypeStruct((rows, 2 * DM), jnp.bfloat16),
        grid=(rows // TILE,),
        in_specs=[
            whole(pending_index),
            whole(pending),
            pl.BlockSpec((TILE, DM), lambda i: (i, 0)),
            whole(w_key),
            whole(w_value),
        ],
        out_specs=pl.BlockSpec((TILE, 2 * DM), lambda i: (i, 0)),
        compiler_params=pltpu.CompilerParams(
            dimension_semantics=("arbitrary",), vmem_limit_bytes=VMEM
        ),
        cost_estimate=pl.CostEstimate(
            flops=17_200_000_000, bytes_accessed=28_000_000, transcendentals=0
        ),
        name="pairs",
    )(pending_index, pending, memory, w_key, w_value)


SEGMENTS = 4


def attend_kernel(blocks, queries, pairs, attended, held, sems):
    step = pl.program_id(0)
    steps = pl.num_programs(0)
    step_slots = held.shape[1] // BR
    capacity = step_slots // SEGMENTS
    segment = capacity * G + META

    def fetch(which, slot):
        for item in range(step_slots):
            first = pl.multiple_of(blocks[which * step_slots + item] * BR, BR)
            pltpu.make_async_copy(
                pairs.at[pl.ds(first, BR), :],
                held.at[slot, pl.ds(item * BR, BR), :],
                sems.at[slot],
            ).start()

    slot = lax.rem(step, 2)

    @pl.when(step == 0)
    def _():
        fetch(0, 0)

    @pl.when(step + 1 < steps)
    def _():
        fetch(step + 1, 1 - slot)

    pltpu.make_async_copy(
        pairs.at[pl.ds(0, step_slots * BR), :], held.at[slot], sems.at[slot]
    ).wait()

    keys_wide = SPAN * BR
    rows_high = SPAN * G
    lane = lax.broadcasted_iota(jnp.int32, (rows_high, keys_wide), 1)
    row = lax.broadcasted_iota(jnp.int32, (rows_high, keys_wide), 0)
    own = (lane // BR) == (row // G)
    offset = lax.rem(lax.broadcasted_iota(jnp.int32, (1, keys_wide), 1), BR).astype(jnp.float32)
    groups = capacity // SPAN
    units = [
        (part, group, head)
        for part in range(SEGMENTS)
        for group in range(groups)
        for head in range(HEADS)
    ]
    scores = []
    for part, group, head in units:
        notes = queries[part * segment + capacity * G : (part + 1) * segment, :].astype(jnp.float32)
        length = notes[0:1, group * keys_wide : (group + 1) * keys_wide]
        usable = own & (offset < length)
        top = part * segment + group * rows_high
        query = queries[top : top + rows_high, head * HEAD_DIM : (head + 1) * HEAD_DIM]
        first = (part * groups + group) * keys_wide
        key = held[slot, first : first + keys_wide, head * HEAD_DIM : (head + 1) * HEAD_DIM]
        score = lax.dot_general(
            query, key, (((1,), (1,)), ((), ())), preferred_element_type=jnp.float32
        ) * (1.0 / 16.0)
        scores.append(jnp.where(usable, score, MASKED))
    scores = jnp.concatenate(scores, 0)
    expons = jnp.exp(scores - jnp.max(scores, axis=1, keepdims=True))
    weights = (expons * (1.0 / jnp.sum(expons, axis=1, keepdims=True))).astype(jnp.bfloat16)
    for number, (part, group, head) in enumerate(units):
        first = (part * groups + group) * keys_wide
        value = held[
            slot, first : first + keys_wide, DM + head * HEAD_DIM : DM + (head + 1) * HEAD_DIM
        ]
        result = jnp.dot(
            weights[number * rows_high : (number + 1) * rows_high],
            value,
            preferred_element_type=jnp.float32,
        )
        top = (part * groups + group) * rows_high
        attended[top : top + rows_high, head * HEAD_DIM : (head + 1) * HEAD_DIM] = result.astype(
            jnp.bfloat16
        )


def attend(blocks, queries, pairs, shards):
    nslots = blocks.shape[0]
    steps = shards // SEGMENTS
    return pl.pallas_call(
        attend_kernel,
        out_shape=jax.ShapeDtypeStruct((nslots * G, DM), jnp.bfloat16),
        grid_spec=pltpu.PrefetchScalarGridSpec(
            num_scalar_prefetch=1,
            grid=(steps,),
            in_specs=[
                pl.BlockSpec((queries.shape[0] // steps, DM), lambda i, b: (i, 0)),
                pl.BlockSpec(memory_space=pl.ANY),
            ],
            out_specs=pl.BlockSpec((nslots * G // steps, DM), lambda i, b: (i, 0)),
            scratch_shapes=[
                pltpu.VMEM((2, nslots // steps * BR, 2 * DM), jnp.bfloat16),
                pltpu.SemaphoreType.DMA((2,)),
            ],
        ),
        compiler_params=pltpu.CompilerParams(
            dimension_semantics=("arbitrary",), vmem_limit_bytes=VMEM
        ),
        cost_estimate=pl.CostEstimate(
            flops=4_000_000_000, bytes_accessed=20_000_000, transcendentals=1_000_000
        ),
        name="attend",
    )(blocks, queries, pairs)


def update_kernel(position, returned, both, fed, kept, source, w_input, fresh, ordered):
    step = pl.program_id(0)
    for item in range(PART // G):
        place = position[step * (PART // G) + item]
        couple = pl.multiple_of((place // 2) * 2 * G, 2 * G)
        rows = returned[pl.ds(couple, 2 * G), :].astype(jnp.float32)
        ordered[item * G : (item + 1) * G, :] = jnp.where(
            lax.rem(place, 2) == 0, rows[:G, :], rows[G:, :]
        )
    for start in range(0, PART, 128):
        rows = slice(start, start + 128)
        attended = ordered[rows, :].astype(jnp.bfloat16)
        gates = jnp.dot(attended, w_input[...], preferred_element_type=jnp.float32)
        reset = jax.nn.sigmoid(gates[:, :DM] + both[rows, :DM])
        update = jax.nn.sigmoid(gates[:, DM : 2 * DM] + both[rows, DM:])
        candidate = jnp.tanh(gates[:, 2 * DM :] + fed[rows, :] + reset * kept[rows, :])
        fresh[rows, :] = (
            (1.0 - update) * candidate + update * source[rows, :].astype(jnp.float32)
        ).astype(jnp.bfloat16)


def updated(position, returned, both, fed, kept, source, w_attended):
    events = source.shape[0]
    return pl.pallas_call(
        update_kernel,
        out_shape=jax.ShapeDtypeStruct((events, DM), jnp.bfloat16),
        grid_spec=pltpu.PrefetchScalarGridSpec(
            num_scalar_prefetch=1,
            grid=(events // PART,),
            in_specs=[
                pl.BlockSpec(returned.shape, lambda i, p: (0, 0)),
                pl.BlockSpec((PART, 2 * DM), lambda i, p: (i, 0)),
                pl.BlockSpec((PART, DM), lambda i, p: (i, 2)),
                pl.BlockSpec((PART, DM), lambda i, p: (i, 2)),
                pl.BlockSpec((PART, DM), lambda i, p: (i, 0)),
                pl.BlockSpec(w_attended.shape, lambda i, p: (0, 0)),
            ],
            out_specs=pl.BlockSpec((PART, DM), lambda i, p: (i, 0)),
            scratch_shapes=[pltpu.VMEM((PART, DM), jnp.float32)],
        ),
        compiler_params=pltpu.CompilerParams(
            dimension_semantics=("arbitrary",), vmem_limit_bytes=VMEM
        ),
        cost_estimate=pl.CostEstimate(
            flops=1_700_000_000, bytes_accessed=15_000_000, transcendentals=1_500_000
        ),
        name="update",
    )(position, returned, both, fed, kept, source, w_attended)


def body(
    memory,
    sectioned_rows,
    sectioned_index,
    src_local,
    messages,
    block_owner,
    block_local,
    block_len,
    w_query,
    w_key,
    w_value,
    w_input,
    w_hidden,
):
    shards = lax.axis_size("mem")
    nblocks = block_local.shape[0]
    capacity = max(2, 2 * nblocks // shards)
    nslots = shards * capacity
    msg = messages.shape[1]

    pending_index = shifted(sectioned_index, "loop", 1)[None, :]
    pending = shifted(sectioned_rows, "loop", 1)

    owners = block_owner[:, 0]
    onehot = (owners[:, None] == jnp.arange(shards, dtype=jnp.int32)[None, :]).astype(jnp.int32)
    rank = jnp.sum((jnp.cumsum(onehot, 0) - onehot) * onehot, 1)
    position = owners * capacity + rank
    unused = (lax.axis_index("mem") * capacity + jnp.arange(nslots, dtype=jnp.int32) % capacity) * 64
    wanted = unused.at[position].set(block_local * 64 + block_len)
    wanted = wanted.reshape(shards, capacity)
    notes = jnp.zeros((shards, META, DM), jnp.int32)
    notes = notes.at[:, 0, : capacity * BR].set(jnp.repeat(wanted % 64, BR, axis=1))
    notes = notes.at[:, 1, :capacity].set(wanted // 64)
    notes = notes.astype(jnp.bfloat16).reshape(shards * META, DM)

    base = memory[src_local]
    queries, source = make_queries(
        position, src_local[:, None], pending_index, pending, base, messages, w_query, notes, nslots
    )
    segment = capacity * G + META
    arrived = lax.all_to_all(
        queries.reshape(shards, segment, DM), "mem", split_axis=0, concat_axis=0, tiled=True
    )
    pairs = make_pairs(pending_index, pending, memory, w_key, w_value)
    blocks = arrived[:, capacity * G + 1, :capacity].astype(jnp.int32).reshape(nslots)
    attended = attend(blocks, arrived.reshape(shards * segment, DM), pairs, shards)
    returned = lax.all_to_all(
        attended.reshape(shards, capacity * G, DM), "mem", split_axis=0, concat_axis=0, tiled=True
    ).reshape(nslots * G, DM)

    fed = jnp.dot(messages, w_input[:msg], preferred_element_type=jnp.float32)
    kept = jnp.dot(source, w_hidden, preferred_element_type=jnp.float32)
    both = fed[:, : 2 * DM] + kept[:, : 2 * DM]
    return updated(position, returned, both, fed, kept, source, w_input[msg:])


def solution(mesh):
    placed = (
        P("mem", None),
        P(("loop", "mem"), None),
        P(("loop", "mem")),
        P(("loop", "mem")),
        P(("loop", "mem"), None),
        P(("loop", "mem"), None),
        P(("loop", "mem")),
        P(("loop", "mem")),
        P(),
        P(),
        P(),
        P(),
        P(),
    )
    return jax.shard_map(
        body, mesh=mesh, in_specs=placed, out_specs=P(("loop", "mem"), None), check_vma=False
    )
```

```python
import jax
import jax.numpy as jnp
from jax import lax
from jax.experimental import pallas as pl
from jax.experimental.pallas import tpu as pltpu
from jax.sharding import PartitionSpec as P

DM = 512
HEADS = 2
HEAD_DIM = 256
BR = 32
G = 8
VMEM = 60 * 1024 * 1024
SMALL = 32 * 1024 * 1024
ATT_VMEM = 32 * 1024 * 1024
SPAN = 8
MASKED = -1e30


def shifted(block, axis, distance):
    size = lax.axis_size(axis)
    route = [((i - distance) % size, i) for i in range(size)]
    return lax.ppermute(block, axis, route)


CHUNK = 128
PART = 128
TILE = 512
META = 16


def query_kernel(
    position,
    source_index,
    pending_index,
    pending,
    base,
    messages,
    w_query,
    notes,
    slots,
    source,
    staged,
    packed,
    kept,
    sems,
):
    events = base.shape[0]
    owners = notes.shape[0] // META
    high = staged.shape[0] // owners
    segment = high + META
    staged[...] = jnp.zeros_like(staged)
    for start in range(0, events, CHUNK):
        rows = slice(start, start + CHUNK)
        same = source_index[rows, :] == pending_index[...]
        chosen = jnp.where(same, 1.0, 0.0)
        hit = jnp.max(chosen, axis=1, keepdims=True) > 0.0
        picked = jnp.dot(
            chosen.astype(jnp.bfloat16), pending[...], preferred_element_type=jnp.float32
        )
        merged = jnp.where(hit, picked, base[rows, :].astype(jnp.float32)).astype(jnp.bfloat16)
        kept[rows, :] = merged
        found = jnp.dot(merged, w_query[:DM, :], preferred_element_type=jnp.float32) + jnp.dot(
            messages[rows, :], w_query[DM:, :], preferred_element_type=jnp.float32
        )
        for item in range(CHUNK // G):
            place = pl.multiple_of(position[start // G + item] * G, G)
            staged[pl.ds(place, G), :] = found[item * G : (item + 1) * G, :]
    copies = []
    parts = 4
    for part in range(parts):
        for owner in range(part * owners // parts, (part + 1) * owners // parts):
            first = owner * segment
            packed[first : first + high, :] = staged[owner * high : (owner + 1) * high, :].astype(
                jnp.bfloat16
            )
            packed[first + high : first + segment, :] = notes[owner * META : (owner + 1) * META, :]
        span = owners // parts * segment
        rows = slice(part * span, (part + 1) * span)
        copies.append(pltpu.make_async_copy(packed.at[rows, :], slots.at[rows, :], sems.at[part]))
        copies[-1].start()
    copies.append(pltpu.make_async_copy(kept, source, sems.at[parts]))
    copies[-1].start()
    for copy in copies:
        copy.wait()


def make_queries(position, source_index, pending_index, pending, base, messages, w_query, notes, nslots):
    events = base.shape[0]
    total = nslots * G + notes.shape[0]
    vmem = pl.BlockSpec(memory_space=pltpu.VMEM)
    out = pl.BlockSpec(memory_space=pltpu.HBM)
    return pl.pallas_call(
        query_kernel,
        out_shape=(
            jax.ShapeDtypeStruct((total, DM), jnp.bfloat16),
            jax.ShapeDtypeStruct((events, DM), jnp.bfloat16),
        ),
        in_specs=[pl.BlockSpec(memory_space=pltpu.SMEM)] + [vmem] * 7,
        out_specs=(out, out),
        scratch_shapes=[
            pltpu.VMEM((nslots * G, DM), jnp.float32),
            pltpu.VMEM((total, DM), jnp.bfloat16),
            pltpu.VMEM((events, DM), jnp.bfloat16),
            pltpu.SemaphoreType.DMA((5,)),
        ],
        compiler_params=pltpu.CompilerParams(vmem_limit_bytes=SMALL),
        cost_estimate=pl.CostEstimate(
            flops=2_000_000_000, bytes_accessed=8_000_000, transcendentals=0
        ),
        name="queries",
    )(position, source_index, pending_index, pending, base, messages, w_query, notes)


def pairs_kernel(pending_index, pending, memory, w_key, w_value, pairs):
    first = pl.program_id(0) * TILE
    row = first + lax.broadcasted_iota(jnp.int32, (TILE, 1), 0)
    chosen = jnp.where(row == pending_index[...], 1.0, 0.0)
    hit = jnp.max(chosen, axis=1, keepdims=True) > 0.0
    picked = jnp.dot(chosen.astype(jnp.bfloat16), pending[...], preferred_element_type=jnp.float32)
    merged = jnp.where(hit, picked, memory[...].astype(jnp.float32)).astype(jnp.bfloat16)
    pairs[:, :DM] = jnp.dot(merged, w_key[...], preferred_element_type=jnp.float32).astype(jnp.bfloat16)
    pairs[:, DM:] = jnp.dot(merged, w_value[...], preferred_element_type=jnp.float32).astype(jnp.bfloat16)


def make_pairs(pending_index, pending, memory, w_key, w_value):
    rows = memory.shape[0]
    whole = lambda array: pl.BlockSpec(array.shape, lambda i: (0, 0))
    return pl.pallas_call(
        pairs_kernel,
        out_shape=jax.ShapeDtypeStruct((rows, 2 * DM), jnp.bfloat16),
        grid=(rows // TILE,),
        in_specs=[
            whole(pending_index),
            whole(pending),
            pl.BlockSpec((TILE, DM), lambda i: (i, 0)),
            whole(w_key),
            whole(w_value),
        ],
        out_specs=pl.BlockSpec((TILE, 2 * DM), lambda i: (i, 0)),
        compiler_params=pltpu.CompilerParams(
            dimension_semantics=("arbitrary",), vmem_limit_bytes=VMEM
        ),
        cost_estimate=pl.CostEstimate(
            flops=17_200_000_000, bytes_accessed=28_000_000, transcendentals=0
        ),
        name="pairs",
    )(pending_index, pending, memory, w_key, w_value)


SEGMENTS = 4


def attend_kernel(queries, pairs, attended, numbers, blocks, sem):
    capacity = pairs.shape[0] // BR // numbers.shape[0]
    shards = numbers.shape[0]
    segment = capacity * G + META
    for part in range(shards):
        first = part * segment + capacity * G
        notes = queries[first : first + META, :128].astype(jnp.float32)
        numbers[part : part + 1, :] = notes[1:2, :].astype(jnp.int32)
    copy = pltpu.make_async_copy(numbers, blocks, sem)
    copy.start()

    keys_wide = SPAN * BR
    rows_high = SPAN * G
    lane = lax.broadcasted_iota(jnp.int32, (rows_high, keys_wide), 1)
    row = lax.broadcasted_iota(jnp.int32, (rows_high, keys_wide), 0)
    own = (lane // BR) == (row // G)
    offset = lax.rem(lax.broadcasted_iota(jnp.int32, (1, keys_wide), 1), BR).astype(jnp.float32)
    groups = capacity // SPAN
    copy.wait()

    @pl.loop(0, shards // SEGMENTS)
    def _(step):
        units = []
        for part in range(SEGMENTS):
            where = step * SEGMENTS + part
            top = pl.multiple_of(where * segment, META)
            notes = queries[pl.ds(top + capacity * G, META), :].astype(jnp.float32)
            for group in range(groups):
                length = notes[0:1, group * keys_wide : (group + 1) * keys_wide]
                usable = own & (offset < length)
                firsts = [
                    pl.multiple_of(blocks[where, group * SPAN + item] * BR, BR)
                    for item in range(SPAN)
                ]
                for head in range(HEADS):
                    units.append((where, top, group, head, usable, firsts))
        scores = []
        for where, top, group, head, usable, firsts in units:
            columns = slice(head * HEAD_DIM, (head + 1) * HEAD_DIM)
            query = queries[pl.ds(top + group * rows_high, rows_high), columns]
            key = jnp.concatenate([pairs[pl.ds(first, BR), columns] for first in firsts], 0)
            score = lax.dot_general(
                query, key, (((1,), (1,)), ((), ())), preferred_element_type=jnp.float32
            ) * (1.0 / 16.0)
            scores.append(jnp.where(usable, score, MASKED))
        scores = jnp.concatenate(scores, 0)
        expons = jnp.exp(scores - jnp.max(scores, axis=1, keepdims=True))
        weights = (expons * (1.0 / jnp.sum(expons, axis=1, keepdims=True))).astype(jnp.bfloat16)
        for number, (where, top, group, head, usable, firsts) in enumerate(units):
            columns = slice(DM + head * HEAD_DIM, DM + (head + 1) * HEAD_DIM)
            value = jnp.concatenate([pairs[pl.ds(first, BR), columns] for first in firsts], 0)
            result = jnp.dot(
                weights[number * rows_high : (number + 1) * rows_high],
                value,
                preferred_element_type=jnp.float32,
            )
            place = pl.multiple_of((where * groups + group) * rows_high, rows_high)
            attended[pl.ds(place, rows_high), head * HEAD_DIM : (head + 1) * HEAD_DIM] = (
                result.astype(jnp.bfloat16)
            )


def attend(queries, pairs, shards, nslots):
    vmem = pl.BlockSpec(memory_space=pltpu.VMEM)
    return pl.pallas_call(
        attend_kernel,
        out_shape=jax.ShapeDtypeStruct((nslots * G, DM), jnp.bfloat16),
        in_specs=[vmem, vmem],
        out_specs=vmem,
        scratch_shapes=[
            pltpu.VMEM((shards, 128), jnp.int32),
            pltpu.SMEM((shards, 128), jnp.int32),
            pltpu.SemaphoreType.DMA,
        ],
        compiler_params=pltpu.CompilerParams(vmem_limit_bytes=ATT_VMEM),
        cost_estimate=pl.CostEstimate(
            flops=4_000_000_000, bytes_accessed=20_000_000, transcendentals=1_000_000
        ),
        name="attend",
    )(queries, pairs)


def update_kernel(position, returned, both, fed, kept, source, w_input, fresh, ordered):
    for start in range(0, source.shape[0], PART):
        rows = slice(start, start + PART)
        for item in range(PART // G):
            place = position[start // G + item]
            couple = pl.multiple_of((place // 2) * 2 * G, 2 * G)
            pair = returned[pl.ds(couple, 2 * G), :].astype(jnp.float32)
            ordered[start + item * G : start + (item + 1) * G, :] = jnp.where(
                lax.rem(place, 2) == 0, pair[:G, :], pair[G:, :]
            )
        attended = ordered[rows, :].astype(jnp.bfloat16)
        gates = jnp.dot(attended, w_input[...], preferred_element_type=jnp.float32)
        reset = jax.nn.sigmoid(gates[:, :DM] + both[rows, :DM])
        update = jax.nn.sigmoid(gates[:, DM : 2 * DM] + both[rows, DM:])
        candidate = jnp.tanh(gates[:, 2 * DM :] + fed[rows, :] + reset * kept[rows, :])
        fresh[rows, :] = (
            (1.0 - update) * candidate + update * source[rows, :].astype(jnp.float32)
        ).astype(jnp.bfloat16)


def updated(position, returned, both, fed, kept, source, w_attended):
    events = source.shape[0]
    vmem = pl.BlockSpec(memory_space=pltpu.VMEM)
    return pl.pallas_call(
        update_kernel,
        out_shape=jax.ShapeDtypeStruct((events, DM), jnp.bfloat16),
        in_specs=[pl.BlockSpec(memory_space=pltpu.SMEM)] + [vmem] * 6,
        out_specs=vmem,
        scratch_shapes=[pltpu.VMEM((events, DM), jnp.float32)],
        compiler_params=pltpu.CompilerParams(vmem_limit_bytes=SMALL),
        cost_estimate=pl.CostEstimate(
            flops=1_700_000_000, bytes_accessed=15_000_000, transcendentals=1_500_000
        ),
        name="update",
    )(position, returned, both, fed, kept, source, w_attended)


def body(
    memory,
    sectioned_rows,
    sectioned_index,
    src_local,
    messages,
    block_owner,
    block_local,
    block_len,
    w_query,
    w_key,
    w_value,
    w_input,
    w_hidden,
):
    shards = lax.axis_size("mem")
    nblocks = block_local.shape[0]
    capacity = max(2, 2 * nblocks // shards)
    nslots = shards * capacity
    msg = messages.shape[1]

    pending_index = shifted(sectioned_index, "loop", 1)[None, :]
    pending = shifted(sectioned_rows, "loop", 1)

    owners = block_owner[:, 0]
    onehot = (owners[:, None] == jnp.arange(shards, dtype=jnp.int32)[None, :]).astype(jnp.int32)
    rank = jnp.sum((jnp.cumsum(onehot, 0) - onehot) * onehot, 1)
    position = owners * capacity + rank
    unused = (lax.axis_index("mem") * capacity + jnp.arange(nslots, dtype=jnp.int32) % capacity) * 64
    wanted = unused.at[position].set(block_local * 64 + block_len)
    wanted = wanted.reshape(shards, capacity)
    notes = jnp.zeros((shards, META, DM), jnp.int32)
    notes = notes.at[:, 0, : capacity * BR].set(jnp.repeat(wanted % 64, BR, axis=1))
    notes = notes.at[:, 1, :capacity].set(wanted // 64)
    notes = notes.astype(jnp.bfloat16).reshape(shards * META, DM)

    base = memory[src_local]
    queries, source = make_queries(
        position, src_local[:, None], pending_index, pending, base, messages, w_query, notes, nslots
    )
    segment = capacity * G + META
    arrived = lax.all_to_all(
        queries.reshape(shards, segment, DM), "mem", split_axis=0, concat_axis=0, tiled=True
    )
    pairs = make_pairs(pending_index, pending, memory, w_key, w_value)
    attended = attend(arrived.reshape(shards * segment, DM), pairs, shards, nslots)
    returned = lax.all_to_all(
        attended.reshape(shards, capacity * G, DM), "mem", split_axis=0, concat_axis=0, tiled=True
    ).reshape(nslots * G, DM)

    fed = jnp.dot(messages, w_input[:msg], preferred_element_type=jnp.float32)
    kept = jnp.dot(source, w_hidden, preferred_element_type=jnp.float32)
    both = fed[:, : 2 * DM] + kept[:, : 2 * DM]
    return updated(
        position, returned, both, fed[:, 2 * DM :], kept[:, 2 * DM :], source, w_input[msg:]
    )


def solution(mesh):
    placed = (
        P("mem", None),
        P(("loop", "mem"), None),
        P(("loop", "mem")),
        P(("loop", "mem")),
        P(("loop", "mem"), None),
        P(("loop", "mem"), None),
        P(("loop", "mem")),
        P(("loop", "mem")),
        P(),
        P(),
        P(),
        P(),
        P(),
    )
    return jax.shard_map(
        body, mesh=mesh, in_specs=placed, out_specs=P(("loop", "mem"), None), check_vma=False
    )
```

```python
import jax
import jax.numpy as jnp
from jax import lax
from jax.experimental import pallas as pl
from jax.experimental.pallas import tpu as pltpu
from jax.sharding import PartitionSpec as P

DM = 512
HEADS = 2
HEAD_DIM = 256
BR = 32
G = 8
SMALL = 24 * 1024 * 1024
ATT_VMEM = 32 * 1024 * 1024
SPAN = 8
MASKED = -1e30


def shifted(block, axis, distance):
    size = lax.axis_size(axis)
    route = [((i - distance) % size, i) for i in range(size)]
    return lax.ppermute(block, axis, route)


CHUNK = 128
PART = 128
TILE = 512
META = 16


def vmem_out(shape, dtype):
    return pltpu.VMEM(shape, dtype)


def hbm_out(shape, dtype):
    return pltpu.HBM(shape, dtype)


def in_hbm(array):
    return pltpu.with_memory_space_constraint(array, pltpu.HBM)


WHOLE = pl.BlockSpec(memory_space=pltpu.VMEM)
THERE = pl.BlockSpec(memory_space=pl.ANY)
SCALARS = pl.BlockSpec(memory_space=pltpu.SMEM)


def prepare_kernel(
    source_index, pending_index, base, messages, w_query, chosen, hit, held, spoken, weight
):
    held[...] = base[...]
    weight[...] = w_query[:DM, :]
    for start in range(0, base.shape[0], CHUNK):
        rows = slice(start, start + CHUNK)
        same = jnp.where(source_index[rows, :] == pending_index[...], 1.0, 0.0)
        chosen[rows, :] = same.astype(jnp.bfloat16)
        hit[rows, :] = jnp.broadcast_to(jnp.max(same, axis=1, keepdims=True), (CHUNK, 128))
        spoken[rows, :] = jnp.dot(
            messages[rows, :], w_query[DM:, :], preferred_element_type=jnp.float32
        )


def prepare(source_index, pending_index, base, messages, w_query):
    events = base.shape[0]
    return pl.pallas_call(
        prepare_kernel,
        out_shape=(
            vmem_out((events, pending_index.shape[1]), jnp.bfloat16),
            vmem_out((events, 128), jnp.float32),
            vmem_out((events, DM), jnp.bfloat16),
            vmem_out((events, DM), jnp.float32),
            vmem_out((DM, DM), jnp.bfloat16),
        ),
        in_specs=[WHOLE] * 5,
        out_specs=(WHOLE,) * 5,
        compiler_params=pltpu.CompilerParams(vmem_limit_bytes=SMALL),
        cost_estimate=pl.CostEstimate(
            flops=300_000_000, bytes_accessed=8_000_000, transcendentals=0
        ),
        name="prepare",
    )(source_index, pending_index, base, messages, w_query)


def query_kernel(
    position,
    chosen,
    hit,
    base,
    spoken,
    w_query,
    notes,
    pending,
    slots,
    source,
    arrived,
    staged,
    packed,
    kept,
    sems,
):
    load = pltpu.make_async_copy(pending, arrived, sems.at[0])
    load.start()
    events = base.shape[0]
    owners = notes.shape[0] // META
    high = staged.shape[0] // owners
    segment = high + META
    staged[...] = jnp.zeros_like(staged)
    load.wait()
    for start in range(0, events, CHUNK):
        rows = slice(start, start + CHUNK)
        picked = jnp.dot(chosen[rows, :], arrived[...], preferred_element_type=jnp.float32)
        merged = jnp.where(
            hit[rows, :1] > 0.0, picked, base[rows, :].astype(jnp.float32)
        ).astype(jnp.bfloat16)
        kept[rows, :] = merged
        found = jnp.dot(merged, w_query[...], preferred_element_type=jnp.float32) + spoken[rows, :]
        for item in range(CHUNK // G):
            place = pl.multiple_of(position[start // G + item] * G, G)
            staged[pl.ds(place, G), :] = found[item * G : (item + 1) * G, :]
    copies = []
    parts = 4
    for part in range(parts):
        for owner in range(part * owners // parts, (part + 1) * owners // parts):
            first = owner * segment
            packed[first : first + high, :] = staged[owner * high : (owner + 1) * high, :].astype(
                jnp.bfloat16
            )
            packed[first + high : first + segment, :] = notes[owner * META : (owner + 1) * META, :]
        span = owners // parts * segment
        rows = slice(part * span, (part + 1) * span)
        copies.append(
            pltpu.make_async_copy(packed.at[rows, :], slots.at[rows, :], sems.at[1 + part])
        )
        copies[-1].start()
    copies.append(pltpu.make_async_copy(kept, source, sems.at[1 + parts]))
    copies[-1].start()
    for copy in copies:
        copy.wait()


def make_queries(position, prepared, notes, pending, nslots):
    events = pending.shape[0]
    total = nslots * G + notes.shape[0]
    return pl.pallas_call(
        query_kernel,
        out_shape=(hbm_out((total, DM), jnp.bfloat16), hbm_out((events, DM), jnp.bfloat16)),
        in_specs=[SCALARS] + [WHOLE] * 6 + [THERE],
        out_specs=(THERE, THERE),
        scratch_shapes=[
            pltpu.VMEM(pending.shape, jnp.bfloat16),
            pltpu.VMEM((nslots * G, DM), jnp.float32),
            pltpu.VMEM((total, DM), jnp.bfloat16),
            pltpu.VMEM((events, DM), jnp.bfloat16),
            pltpu.SemaphoreType.DMA((6,)),
        ],
        compiler_params=pltpu.CompilerParams(vmem_limit_bytes=SMALL),
        cost_estimate=pl.CostEstimate(
            flops=2_000_000_000, bytes_accessed=8_000_000, transcendentals=0
        ),
        name="queries",
    )(position, *prepared, notes, in_hbm(pending))


def pairs_kernel(pending_index, w_key, w_value, pending, memory, pairs, arrived, tiles, sems):
    load = pltpu.make_async_copy(pending, arrived, sems.at[2])
    load.start()
    steps = memory.shape[0] // TILE

    def fetch(step, slot):
        first = pl.multiple_of(step * TILE, TILE)
        return pltpu.make_async_copy(
            memory.at[pl.ds(first, TILE), :], tiles.at[slot], sems.at[slot]
        )

    fetch(0, 0).start()
    load.wait()

    @pl.loop(0, steps)
    def _(step):
        slot = lax.rem(step, 2)

        @pl.when(step + 1 < steps)
        def _():
            fetch(step + 1, 1 - slot).start()

        fetch(step, slot).wait()
        first = pl.multiple_of(step * TILE, TILE)
        row = first + lax.broadcasted_iota(jnp.int32, (TILE, 1), 0)
        chosen = jnp.where(row == pending_index[...], 1.0, 0.0)
        hit = jnp.max(chosen, axis=1, keepdims=True) > 0.0
        picked = jnp.dot(
            chosen.astype(jnp.bfloat16), arrived[...], preferred_element_type=jnp.float32
        )
        merged = jnp.where(hit, picked, tiles[slot].astype(jnp.float32)).astype(jnp.bfloat16)
        rows = pl.ds(first, TILE)
        pairs[rows, :DM] = jnp.dot(
            merged, w_key[...], preferred_element_type=jnp.float32
        ).astype(jnp.bfloat16)
        pairs[rows, DM:] = jnp.dot(
            merged, w_value[...], preferred_element_type=jnp.float32
        ).astype(jnp.bfloat16)


def make_pairs(pending_index, pending, memory, w_key, w_value):
    rows = memory.shape[0]
    return pl.pallas_call(
        pairs_kernel,
        out_shape=vmem_out((rows, 2 * DM), jnp.bfloat16),
        in_specs=[WHOLE] * 3 + [THERE] * 2,
        out_specs=WHOLE,
        scratch_shapes=[
            pltpu.VMEM(pending.shape, jnp.bfloat16),
            pltpu.VMEM((2, TILE, DM), jnp.bfloat16),
            pltpu.SemaphoreType.DMA((3,)),
        ],
        compiler_params=pltpu.CompilerParams(vmem_limit_bytes=ATT_VMEM),
        cost_estimate=pl.CostEstimate(
            flops=17_200_000_000, bytes_accessed=28_000_000, transcendentals=0
        ),
        name="pairs",
    )(pending_index, w_key, w_value, in_hbm(pending), in_hbm(memory))


SEGMENTS = 4


def attend_kernel(pairs, queries, attended, held, notes, result, numbers, blocks, sems):
    capacity = pairs.shape[0] // BR // numbers.shape[0]
    shards = numbers.shape[0]
    segment = capacity * G + META
    batches = shards // SEGMENTS
    marks = []
    for part in range(shards):
        first = part * segment + capacity * G
        marks.append(
            pltpu.make_async_copy(
                queries.at[first : first + META, :],
                notes.at[part * META : (part + 1) * META, :],
                sems.at[0],
            )
        )
        marks[-1].start()
    for batch in range(batches):
        rows = pl.ds(batch * SEGMENTS * segment, SEGMENTS * segment)
        pltpu.make_async_copy(queries.at[rows, :], held.at[rows, :], sems.at[1 + batch]).start()
    pltpu.make_async_copy(queries.at[: shards * META, :], notes, sems.at[0]).wait()
    for part in range(shards):
        numbers[part : part + 1, :] = (
            notes[part * META : (part + 1) * META, :128].astype(jnp.float32)[1:2, :].astype(jnp.int32)
        )
    copy = pltpu.make_async_copy(numbers, blocks, sems.at[0])
    copy.start()

    keys_wide = SPAN * BR
    rows_high = SPAN * G
    lane = lax.broadcasted_iota(jnp.int32, (rows_high, keys_wide), 1)
    row = lax.broadcasted_iota(jnp.int32, (rows_high, keys_wide), 0)
    own = (lane // BR) == (row // G)
    offset = lax.rem(lax.broadcasted_iota(jnp.int32, (1, keys_wide), 1), BR).astype(jnp.float32)
    groups = capacity // SPAN
    copy.wait()

    @pl.loop(0, batches)
    def _(step):
        area = pl.multiple_of(step * SEGMENTS * segment, META)
        pltpu.make_async_copy(
            queries.at[pl.ds(area, SEGMENTS * segment), :],
            held.at[pl.ds(area, SEGMENTS * segment), :],
            sems.at[1 + step],
        ).wait()
        units = []
        for part in range(SEGMENTS):
            where = step * SEGMENTS + part
            top = pl.multiple_of(where * segment, META)
            told = held[pl.ds(top + capacity * G, META), :].astype(jnp.float32)
            for group in range(groups):
                length = told[0:1, group * keys_wide : (group + 1) * keys_wide]
                usable = own & (offset < length)
                firsts = [
                    pl.multiple_of(blocks[where, group * SPAN + item] * BR, BR)
                    for item in range(SPAN)
                ]
                for head in range(HEADS):
                    units.append((where, top, group, head, usable, firsts))
        scores = []
        for where, top, group, head, usable, firsts in units:
            columns = slice(head * HEAD_DIM, (head + 1) * HEAD_DIM)
            query = held[pl.ds(top + group * rows_high, rows_high), columns]
            key = jnp.concatenate([pairs[pl.ds(first, BR), columns] for first in firsts], 0)
            score = lax.dot_general(
                query, key, (((1,), (1,)), ((), ())), preferred_element_type=jnp.float32
            ) * (1.0 / 16.0)
            scores.append(jnp.where(usable, score, MASKED))
        scores = jnp.concatenate(scores, 0)
        expons = jnp.exp(scores - jnp.max(scores, axis=1, keepdims=True))
        weights = (expons * (1.0 / jnp.sum(expons, axis=1, keepdims=True))).astype(jnp.bfloat16)
        for number, (where, top, group, head, usable, firsts) in enumerate(units):
            columns = slice(DM + head * HEAD_DIM, DM + (head + 1) * HEAD_DIM)
            value = jnp.concatenate([pairs[pl.ds(first, BR), columns] for first in firsts], 0)
            answer = jnp.dot(
                weights[number * rows_high : (number + 1) * rows_high],
                value,
                preferred_element_type=jnp.float32,
            )
            place = pl.multiple_of((where * groups + group) * rows_high, rows_high)
            result[pl.ds(place, rows_high), head * HEAD_DIM : (head + 1) * HEAD_DIM] = (
                answer.astype(jnp.bfloat16)
            )
        batch_rows = SEGMENTS * capacity * G
        done = pl.ds(pl.multiple_of(step * batch_rows, batch_rows), batch_rows)
        pltpu.make_async_copy(result.at[done, :], attended.at[done, :], sems.at[1 + batches]).start()

    pltpu.make_async_copy(result, attended, sems.at[1 + batches]).wait()


def attend(queries, pairs, shards, nslots):
    return pl.pallas_call(
        attend_kernel,
        out_shape=hbm_out((nslots * G, DM), jnp.bfloat16),
        in_specs=[WHOLE, THERE],
        out_specs=THERE,
        scratch_shapes=[
            pltpu.VMEM(queries.shape, jnp.bfloat16),
            pltpu.VMEM((shards * META, DM), jnp.bfloat16),
            pltpu.VMEM((nslots * G, DM), jnp.bfloat16),
            pltpu.VMEM((shards, 128), jnp.int32),
            pltpu.SMEM((shards, 128), jnp.int32),
            pltpu.SemaphoreType.DMA((2 + shards // SEGMENTS,)),
        ],
        compiler_params=pltpu.CompilerParams(vmem_limit_bytes=ATT_VMEM),
        cost_estimate=pl.CostEstimate(
            flops=4_000_000_000, bytes_accessed=20_000_000, transcendentals=1_000_000
        ),
        name="attend",
    )(pairs, in_hbm(queries))


def gate_kernel(messages, source, w_input, w_hidden, both, fed, kept, held, weight):
    msg = messages.shape[1]
    held[...] = source[...]
    weight[...] = w_input[msg:, :]
    for start in range(0, source.shape[0], 256):
        rows = slice(start, start + 256)
        spoken = jnp.dot(messages[rows, :], w_input[:msg, :], preferred_element_type=jnp.float32)
        hidden = jnp.dot(source[rows, :], w_hidden[...], preferred_element_type=jnp.float32)
        both[rows, :] = spoken[:, : 2 * DM] + hidden[:, : 2 * DM]
        fed[rows, :] = spoken[:, 2 * DM :]
        kept[rows, :] = hidden[:, 2 * DM :]


def make_gates(messages, source, w_input, w_hidden):
    events, msg = messages.shape
    return pl.pallas_call(
        gate_kernel,
        out_shape=(
            vmem_out((events, 2 * DM), jnp.float32),
            vmem_out((events, DM), jnp.float32),
            vmem_out((events, DM), jnp.float32),
            vmem_out((events, DM), jnp.bfloat16),
            vmem_out((w_input.shape[0] - msg, 3 * DM), jnp.bfloat16),
        ),
        in_specs=[WHOLE] * 4,
        out_specs=(WHOLE,) * 5,
        compiler_params=pltpu.CompilerParams(vmem_limit_bytes=SMALL),
        cost_estimate=pl.CostEstimate(
            flops=2_400_000_000, bytes_accessed=15_000_000, transcendentals=0
        ),
        name="gates",
    )(messages, source, w_input, w_hidden)


def update_kernel(
    position, both, fed, kept, source, w_input, returned, fresh, arrived, ordered, result, sems
):
    load = pltpu.make_async_copy(returned, arrived, sems.at[0])
    load.start()
    load.wait()
    copies = []
    for start in range(0, source.shape[0], PART):
        rows = slice(start, start + PART)
        for item in range(PART // G):
            place = position[start // G + item]
            couple = pl.multiple_of((place // 2) * 2 * G, 2 * G)
            pair = arrived[pl.ds(couple, 2 * G), :].astype(jnp.float32)
            ordered[start + item * G : start + (item + 1) * G, :] = jnp.where(
                lax.rem(place, 2) == 0, pair[:G, :], pair[G:, :]
            )
        attended = ordered[rows, :].astype(jnp.bfloat16)
        gates = jnp.dot(attended, w_input[...], preferred_element_type=jnp.float32)
        reset = jax.nn.sigmoid(gates[:, :DM] + both[rows, :DM])
        update = jax.nn.sigmoid(gates[:, DM : 2 * DM] + both[rows, DM:])
        candidate = jnp.tanh(gates[:, 2 * DM :] + fed[rows, :] + reset * kept[rows, :])
        result[rows, :] = (
            (1.0 - update) * candidate + update * source[rows, :].astype(jnp.float32)
        ).astype(jnp.bfloat16)
        copies.append(
            pltpu.make_async_copy(
                result.at[rows, :], fresh.at[rows, :], sems.at[1 + start // PART]
            )
        )
        copies[-1].start()
    for copy in copies:
        copy.wait()


def updated(position, returned, gates):
    events = gates[3].shape[0]
    return pl.pallas_call(
        update_kernel,
        out_shape=hbm_out((events, DM), jnp.bfloat16),
        in_specs=[SCALARS] + [WHOLE] * 5 + [THERE],
        out_specs=THERE,
        scratch_shapes=[
            pltpu.VMEM(returned.shape, jnp.bfloat16),
            pltpu.VMEM((events, DM), jnp.float32),
            pltpu.VMEM((events, DM), jnp.bfloat16),
            pltpu.SemaphoreType.DMA((1 + events // PART,)),
        ],
        compiler_params=pltpu.CompilerParams(vmem_limit_bytes=SMALL),
        cost_estimate=pl.CostEstimate(
            flops=1_700_000_000, bytes_accessed=15_000_000, transcendentals=1_500_000
        ),
        name="update",
    )(position, *gates, in_hbm(returned))


def body(
    memory,
    sectioned_rows,
    sectioned_index,
    src_local,
    messages,
    block_owner,
    block_local,
    block_len,
    w_query,
    w_key,
    w_value,
    w_input,
    w_hidden,
):
    shards = lax.axis_size("mem")
    nblocks = block_local.shape[0]
    capacity = max(2, 2 * nblocks // shards)
    nslots = shards * capacity

    pending_index = shifted(sectioned_index, "loop", 1)[None, :]
    pending = shifted(sectioned_rows, "loop", 1)

    owners = block_owner[:, 0]
    onehot = (owners[:, None] == jnp.arange(shards, dtype=jnp.int32)[None, :]).astype(jnp.int32)
    rank = jnp.sum((jnp.cumsum(onehot, 0) - onehot) * onehot, 1)
    position = owners * capacity + rank
    unused = (lax.axis_index("mem") * capacity + jnp.arange(nslots, dtype=jnp.int32) % capacity) * 64
    wanted = unused.at[position].set(block_local * 64 + block_len)
    wanted = wanted.reshape(shards, capacity)
    notes = jnp.zeros((shards, META, DM), jnp.int32)
    notes = notes.at[:, 0, : capacity * BR].set(jnp.repeat(wanted % 64, BR, axis=1))
    notes = notes.at[:, 1, :capacity].set(wanted // 64)
    notes = notes.astype(jnp.bfloat16).reshape(shards * META, DM)

    base = memory[src_local]
    prepared = prepare(src_local[:, None], pending_index, base, messages, w_query)
    queries, source = make_queries(position, prepared, notes, pending, nslots)
    segment = capacity * G + META
    arrived = lax.all_to_all(
        queries.reshape(shards, segment, DM), "mem", split_axis=0, concat_axis=0, tiled=True
    )
    pairs = make_pairs(pending_index, pending, memory, w_key, w_value)
    attended = attend(arrived.reshape(shards * segment, DM), pairs, shards, nslots)
    returned = lax.all_to_all(
        attended.reshape(shards, capacity * G, DM), "mem", split_axis=0, concat_axis=0, tiled=True
    ).reshape(nslots * G, DM)

    gates = make_gates(messages, source, w_input, w_hidden)
    return updated(position, returned, gates)


def solution(mesh):
    placed = (
        P("mem", None),
        P(("loop", "mem"), None),
        P(("loop", "mem")),
        P(("loop", "mem")),
        P(("loop", "mem"), None),
        P(("loop", "mem"), None),
        P(("loop", "mem")),
        P(("loop", "mem")),
        P(),
        P(),
        P(),
        P(),
        P(),
    )
    return jax.shard_map(
        body, mesh=mesh, in_specs=placed, out_specs=P(("loop", "mem"), None), check_vma=False
    )
```

```python
import jax
import jax.numpy as jnp
from jax import lax
from jax.experimental import pallas as pl
from jax.experimental.pallas import tpu as pltpu
from jax.sharding import PartitionSpec as P

DM = 512
HEADS = 2
HEAD_DIM = 256
BR = 32
G = 8
SMALL = 24 * 1024 * 1024
LARGE = 56 * 1024 * 1024
SPAN = 8
MASKED = -1e30


def shifted(block, axis, distance):
    size = lax.axis_size(axis)
    route = [((i - distance) % size, i) for i in range(size)]
    return lax.ppermute(block, axis, route)


CHUNK = 256
PART = 128
TILE = 512
META = 16


def vmem_out(shape, dtype):
    return pltpu.VMEM(shape, dtype)


def hbm_out(shape, dtype):
    return pltpu.HBM(shape, dtype)


def in_hbm(array):
    return pltpu.with_memory_space_constraint(array, pltpu.HBM)


WHOLE = pl.BlockSpec(memory_space=pltpu.VMEM)
THERE = pl.BlockSpec(memory_space=pl.ANY)
SCALARS = pl.BlockSpec(memory_space=pltpu.SMEM)


def prepare_kernel(
    source_index, pending_index, base, messages, w_query, chosen, hit, held, spoken, weight
):
    held[...] = base[...]
    weight[...] = w_query[:DM, :]
    for start in range(0, base.shape[0], CHUNK):
        rows = slice(start, start + CHUNK)
        same = jnp.where(source_index[rows, :] == pending_index[...], 1.0, 0.0)
        chosen[rows, :] = same.astype(jnp.bfloat16)
        hit[rows, :] = jnp.broadcast_to(jnp.max(same, axis=1, keepdims=True), (CHUNK, 128))
        spoken[rows, :] = jnp.dot(
            messages[rows, :], w_query[DM:, :], preferred_element_type=jnp.float32
        )


def prepare(source_index, pending_index, base, messages, w_query):
    events = base.shape[0]
    return pl.pallas_call(
        prepare_kernel,
        out_shape=(
            vmem_out((events, pending_index.shape[1]), jnp.bfloat16),
            vmem_out((events, 128), jnp.float32),
            vmem_out((events, DM), jnp.bfloat16),
            vmem_out((events, DM), jnp.float32),
            vmem_out((DM, DM), jnp.bfloat16),
        ),
        in_specs=[WHOLE] * 5,
        out_specs=(WHOLE,) * 5,
        compiler_params=pltpu.CompilerParams(vmem_limit_bytes=SMALL),
        cost_estimate=pl.CostEstimate(
            flops=300_000_000, bytes_accessed=8_000_000, transcendentals=0
        ),
        name="prepare",
    )(source_index, pending_index, base, messages, w_query)


def query_kernel(
    position,
    chosen,
    hit,
    base,
    spoken,
    w_query,
    notes,
    pending,
    slots,
    source,
    arrived,
    staged,
    packed,
    kept,
    sems,
):
    load = pltpu.make_async_copy(pending, arrived, sems.at[0])
    load.start()
    events = base.shape[0]
    owners = notes.shape[0] // META
    high = staged.shape[0] // owners
    segment = high + META
    staged[...] = jnp.zeros_like(staged)
    load.wait()
    for start in range(0, events, CHUNK):
        rows = slice(start, start + CHUNK)
        picked = jnp.dot(chosen[rows, :], arrived[...], preferred_element_type=jnp.float32)
        merged = jnp.where(
            hit[rows, :1] > 0.0, picked, base[rows, :].astype(jnp.float32)
        ).astype(jnp.bfloat16)
        kept[rows, :] = merged
        found = jnp.dot(merged, w_query[...], preferred_element_type=jnp.float32) + spoken[rows, :]
        for item in range(CHUNK // G):
            place = pl.multiple_of(position[start // G + item] * G, G)
            staged[pl.ds(place, G), :] = found[item * G : (item + 1) * G, :]
    copies = []
    parts = 4
    for part in range(parts):
        for owner in range(part * owners // parts, (part + 1) * owners // parts):
            first = owner * segment
            packed[first : first + high, :] = staged[owner * high : (owner + 1) * high, :].astype(
                jnp.bfloat16
            )
            packed[first + high : first + segment, :] = notes[owner * META : (owner + 1) * META, :]
        span = owners // parts * segment
        rows = slice(part * span, (part + 1) * span)
        copies.append(
            pltpu.make_async_copy(packed.at[rows, :], slots.at[rows, :], sems.at[1 + part])
        )
        copies[-1].start()
    copies.append(pltpu.make_async_copy(kept, source, sems.at[1 + parts]))
    copies[-1].start()
    for copy in copies:
        copy.wait()


def make_queries(position, prepared, notes, pending, nslots):
    events = pending.shape[0]
    total = nslots * G + notes.shape[0]
    return pl.pallas_call(
        query_kernel,
        out_shape=(hbm_out((total, DM), jnp.bfloat16), hbm_out((events, DM), jnp.bfloat16)),
        in_specs=[SCALARS] + [WHOLE] * 6 + [THERE],
        out_specs=(THERE, THERE),
        scratch_shapes=[
            pltpu.VMEM(pending.shape, jnp.bfloat16),
            pltpu.VMEM((nslots * G, DM), jnp.float32),
            pltpu.VMEM((total, DM), jnp.bfloat16),
            pltpu.VMEM((events, DM), jnp.bfloat16),
            pltpu.SemaphoreType.DMA((6,)),
        ],
        compiler_params=pltpu.CompilerParams(vmem_limit_bytes=SMALL),
        cost_estimate=pl.CostEstimate(
            flops=2_000_000_000, bytes_accessed=8_000_000, transcendentals=0
        ),
        name="queries",
    )(position, *prepared, notes, in_hbm(pending))


def pairs_kernel(pending_index, pending, memory, w_key, w_value, *pairs):
    first = pl.program_id(0) * TILE
    row = first + lax.broadcasted_iota(jnp.int32, (TILE, 1), 0)
    chosen = jnp.where(row == pending_index[...], 1.0, 0.0)
    hit = jnp.max(chosen, axis=1, keepdims=True) > 0.0
    picked = jnp.dot(chosen.astype(jnp.bfloat16), pending[...], preferred_element_type=jnp.float32)
    merged = jnp.where(hit, picked, memory[...].astype(jnp.float32)).astype(jnp.bfloat16)
    for weight, part in ((w_key, pairs[:HEADS]), (w_value, pairs[HEADS:])):
        rows = jnp.dot(merged, weight[...], preferred_element_type=jnp.float32).astype(jnp.bfloat16)
        for head in range(HEADS):
            part[head][...] = rows[:, head * HEAD_DIM : (head + 1) * HEAD_DIM]


def make_pairs(pending_index, pending, memory, w_key, w_value):
    rows = memory.shape[0]
    whole = lambda array: pl.BlockSpec(array.shape, lambda i: (0, 0))
    return pl.pallas_call(
        pairs_kernel,
        out_shape=(jax.ShapeDtypeStruct((rows, HEAD_DIM), jnp.bfloat16),) * (2 * HEADS),
        grid=(rows // TILE,),
        in_specs=[
            whole(pending_index),
            whole(pending),
            pl.BlockSpec((TILE, DM), lambda i: (i, 0)),
            whole(w_key),
            whole(w_value),
        ],
        out_specs=(pl.BlockSpec((TILE, HEAD_DIM), lambda i: (i, 0)),) * (2 * HEADS),
        compiler_params=pltpu.CompilerParams(
            dimension_semantics=("arbitrary",), vmem_limit_bytes=LARGE
        ),
        cost_estimate=pl.CostEstimate(
            flops=17_200_000_000, bytes_accessed=28_000_000, transcendentals=0
        ),
        name="pairs",
    )(pending_index, pending, memory, w_key, w_value)


SEGMENTS = 8


def attend_kernel(
    queries, key_0, key_1, value_0, value_1, attended, held, notes, weights, result, numbers, blocks, *rest
):
    pairs, sems = rest[: 2 * HEADS], rest[2 * HEADS]
    capacity = key_0.shape[0] // BR // numbers.shape[0]
    shards = numbers.shape[0]
    segment = capacity * G + META
    batches = shards // SEGMENTS
    for part in range(shards):
        first = part * segment + capacity * G
        pltpu.make_async_copy(
            queries.at[first : first + META, :],
            notes.at[part * META : (part + 1) * META, :],
            sems.at[0],
        ).start()
    load = pltpu.make_async_copy(queries, held, sems.at[1])
    loads = [
        pltpu.make_async_copy(there, here, sems.at[2 + number])
        for number, (there, here) in enumerate(zip((key_0, key_1, value_0, value_1), pairs))
    ]
    loads[0].start()
    load.start()
    for copy in loads[1:]:
        copy.start()
    pltpu.make_async_copy(queries.at[: shards * META, :], notes, sems.at[0]).wait()
    for part in range(shards):
        numbers[part : part + 1, :] = (
            notes[part * META : (part + 1) * META, :128].astype(jnp.float32)[1:2, :].astype(jnp.int32)
        )
    copy = pltpu.make_async_copy(numbers, blocks, sems.at[0])
    copy.start()

    keys_wide = SPAN * BR
    rows_high = SPAN * G
    lane = lax.broadcasted_iota(jnp.int32, (rows_high, keys_wide), 1)
    row = lax.broadcasted_iota(jnp.int32, (rows_high, keys_wide), 0)
    own = (lane // BR) == (row // G)
    offset = lax.rem(lax.broadcasted_iota(jnp.int32, (1, keys_wide), 1), BR).astype(jnp.float32)
    groups = capacity // SPAN
    batch_groups = SEGMENTS * groups
    batch_rows = batch_groups * rows_high
    copy.wait()
    load.wait()

    def slices(array, step, part, group):
        where = step * SEGMENTS + part
        return jnp.concatenate(
            [
                array[pl.ds(pl.multiple_of(blocks[where, group * SPAN + item] * BR, BR), BR), :]
                for item in range(SPAN)
            ],
            0,
        )

    for head in range(HEADS):
        columns = slice(head * HEAD_DIM, (head + 1) * HEAD_DIM)
        loads[head].wait()

        @pl.loop(0, batches)
        def _(step):
            scores = []
            for part in range(SEGMENTS):
                top = pl.multiple_of((step * SEGMENTS + part) * segment, META)
                told = held[pl.ds(top + capacity * G, META), :].astype(jnp.float32)
                for group in range(groups):
                    length = told[0:1, group * keys_wide : (group + 1) * keys_wide]
                    usable = own & (offset < length)
                    query = held[pl.ds(top + group * rows_high, rows_high), columns]
                    score = lax.dot_general(
                        query,
                        slices(pairs[head], step, part, group),
                        (((1,), (1,)), ((), ())),
                        preferred_element_type=jnp.float32,
                    ) * (1.0 / 16.0)
                    scores.append(jnp.where(usable, score, MASKED))
            scores = jnp.concatenate(scores, 0)
            expons = jnp.exp(scores - jnp.max(scores, axis=1, keepdims=True))
            first = pl.multiple_of(step * batch_rows, batch_rows)
            weights[head, pl.ds(first, batch_rows), :] = (
                expons * (1.0 / jnp.sum(expons, axis=1, keepdims=True))
            ).astype(jnp.bfloat16)

    for head in range(HEADS):
        columns = slice(head * HEAD_DIM, (head + 1) * HEAD_DIM)
        loads[HEADS + head].wait()

        @pl.loop(0, batches)
        def _(step):
            for part in range(SEGMENTS):
                for group in range(groups):
                    place = step * batch_rows + (part * groups + group) * rows_high
                    rows = pl.ds(pl.multiple_of(place, rows_high), rows_high)
                    result[rows, columns] = jnp.dot(
                        weights[head, rows, :],
                        slices(pairs[HEADS + head], step, part, group),
                        preferred_element_type=jnp.float32,
                    ).astype(jnp.bfloat16)
            if head == HEADS - 1:
                done = pl.ds(pl.multiple_of(step * batch_rows, batch_rows), batch_rows)
                pltpu.make_async_copy(result.at[done, :], attended.at[done, :], sems.at[0]).start()

    pltpu.make_async_copy(result, attended, sems.at[0]).wait()


def attend(queries, pairs, shards, nslots):
    return pl.pallas_call(
        attend_kernel,
        out_shape=hbm_out((nslots * G, DM), jnp.bfloat16),
        in_specs=[THERE] * (1 + 2 * HEADS),
        out_specs=THERE,
        scratch_shapes=[
            pltpu.VMEM(queries.shape, jnp.bfloat16),
            pltpu.VMEM((shards * META, DM), jnp.bfloat16),
            pltpu.VMEM((HEADS, nslots * G, SPAN * BR), jnp.bfloat16),
            pltpu.VMEM((nslots * G, DM), jnp.bfloat16),
            pltpu.VMEM((shards, 128), jnp.int32),
            pltpu.SMEM((shards, 128), jnp.int32),
        ]
        + [pltpu.VMEM(array.shape, jnp.bfloat16) for array in pairs]
        + [pltpu.SemaphoreType.DMA((2 + 2 * HEADS,))],
        compiler_params=pltpu.CompilerParams(vmem_limit_bytes=LARGE),
        cost_estimate=pl.CostEstimate(
            flops=4_000_000_000, bytes_accessed=20_000_000, transcendentals=1_000_000
        ),
        name="attend",
    )(in_hbm(queries), *[in_hbm(array) for array in pairs])


def gate_kernel(messages, source, w_input, w_hidden, sums):
    msg = messages.shape[1]
    spoken = jnp.dot(messages[...], w_input[:msg, :], preferred_element_type=jnp.float32)
    hidden = jnp.dot(source[...], w_hidden[...], preferred_element_type=jnp.float32)
    sums[:, : 2 * DM] = spoken[:, : 2 * DM] + hidden[:, : 2 * DM]
    sums[:, 2 * DM : 3 * DM] = spoken[:, 2 * DM :]
    sums[:, 3 * DM :] = hidden[:, 2 * DM :]


def make_gates(messages, source, w_input, w_hidden):
    events, msg = messages.shape
    high = 256
    whole = lambda array: pl.BlockSpec(array.shape, lambda i: (0, 0))
    part = lambda wide: pl.BlockSpec((high, wide), lambda i: (i, 0))
    return pl.pallas_call(
        gate_kernel,
        out_shape=jax.ShapeDtypeStruct((events, 4 * DM), jnp.float32),
        grid=(events // high,),
        in_specs=[part(msg), part(DM), whole(w_input), whole(w_hidden)],
        out_specs=part(4 * DM),
        compiler_params=pltpu.CompilerParams(
            dimension_semantics=("arbitrary",), vmem_limit_bytes=LARGE
        ),
        cost_estimate=pl.CostEstimate(
            flops=2_400_000_000, bytes_accessed=15_000_000, transcendentals=0
        ),
        name="gates",
    )(messages, source, w_input, w_hidden)


LOADED = 256


def update_kernel(
    position,
    returned,
    sums,
    source,
    w_input,
    fresh,
    arrived,
    sums_here,
    source_here,
    weight,
    ordered,
    result,
    sems,
):
    events = source.shape[0]
    base = w_input.shape[0] - weight.shape[0]
    pieces = events // LOADED
    first_loads = [
        pltpu.make_async_copy(returned, arrived, sems.at[0]),
        pltpu.make_async_copy(w_input.at[base:, :], weight, sems.at[1]),
        pltpu.make_async_copy(source, source_here, sems.at[2]),
    ]
    loads = []
    for piece in range(pieces):
        rows = slice(piece * LOADED, (piece + 1) * LOADED)
        loads.append(
            pltpu.make_async_copy(sums.at[rows, :], sums_here.at[rows, :], sems.at[3 + piece])
        )
    for copy in first_loads[:2] + loads[:1] + first_loads[2:] + loads[1:]:
        copy.start()
    copies = []
    first_loads[0].wait()
    for number in range(events // PART):
        rows = slice(number * PART, (number + 1) * PART)
        for item in range(PART // G):
            place = position[number * (PART // G) + item]
            couple = pl.multiple_of((place // 2) * 2 * G, 2 * G)
            pair = arrived[pl.ds(couple, 2 * G), :].astype(jnp.float32)
            top = number * PART + item * G
            ordered[top : top + G, :] = jnp.where(
                lax.rem(place, 2) == 0, pair[:G, :], pair[G:, :]
            )
        if number == 0:
            first_loads[1].wait()
        attended = ordered[rows, :].astype(jnp.bfloat16)
        gates = jnp.dot(attended, weight[...], preferred_element_type=jnp.float32)
        if number * PART % LOADED == 0:
            loads[number * PART // LOADED].wait()
        if number == 0:
            first_loads[2].wait()
        reset = jax.nn.sigmoid(gates[:, :DM] + sums_here[rows, :DM])
        update = jax.nn.sigmoid(gates[:, DM : 2 * DM] + sums_here[rows, DM : 2 * DM])
        candidate = jnp.tanh(
            gates[:, 2 * DM :] + sums_here[rows, 2 * DM : 3 * DM] + reset * sums_here[rows, 3 * DM :]
        )
        result[rows, :] = (
            (1.0 - update) * candidate + update * source_here[rows, :].astype(jnp.float32)
        ).astype(jnp.bfloat16)
        copies.append(
            pltpu.make_async_copy(
                result.at[rows, :], fresh.at[rows, :], sems.at[3 + pieces + number]
            )
        )
        copies[-1].start()
    for copy in copies:
        copy.wait()


def updated(position, returned, sums, source, w_input):
    events = source.shape[0]
    operands = (returned, sums, source, w_input)
    return pl.pallas_call(
        update_kernel,
        out_shape=hbm_out((events, DM), jnp.bfloat16),
        in_specs=[SCALARS] + [THERE] * 4,
        out_specs=THERE,
        scratch_shapes=[
            pltpu.VMEM(returned.shape, jnp.bfloat16),
            pltpu.VMEM(sums.shape, jnp.float32),
            pltpu.VMEM(source.shape, jnp.bfloat16),
            pltpu.VMEM((DM, 3 * DM), jnp.bfloat16),
            pltpu.VMEM((events, DM), jnp.float32),
            pltpu.VMEM((events, DM), jnp.bfloat16),
            pltpu.SemaphoreType.DMA((3 + events // LOADED + events // PART,)),
        ],
        compiler_params=pltpu.CompilerParams(vmem_limit_bytes=LARGE),
        cost_estimate=pl.CostEstimate(
            flops=1_700_000_000, bytes_accessed=15_000_000, transcendentals=1_500_000
        ),
        name="update",
    )(position, *[in_hbm(array) for array in operands])


def body(
    memory,
    sectioned_rows,
    sectioned_index,
    src_local,
    messages,
    block_owner,
    block_local,
    block_len,
    w_query,
    w_key,
    w_value,
    w_input,
    w_hidden,
):
    shards = lax.axis_size("mem")
    nblocks = block_local.shape[0]
    capacity = max(2, 2 * nblocks // shards)
    nslots = shards * capacity

    pending_index = shifted(sectioned_index, "loop", 1)[None, :]
    pending = shifted(sectioned_rows, "loop", 1)

    owners = block_owner[:, 0]
    onehot = (owners[:, None] == jnp.arange(shards, dtype=jnp.int32)[None, :]).astype(jnp.int32)
    rank = jnp.sum((jnp.cumsum(onehot, 0) - onehot) * onehot, 1)
    position = owners * capacity + rank
    unused = (lax.axis_index("mem") * capacity + jnp.arange(nslots, dtype=jnp.int32) % capacity) * 64
    wanted = unused.at[position].set(block_local * 64 + block_len)
    wanted = wanted.reshape(shards, capacity)
    notes = jnp.zeros((shards, META, DM), jnp.int32)
    notes = notes.at[:, 0, : capacity * BR].set(jnp.repeat(wanted % 64, BR, axis=1))
    notes = notes.at[:, 1, :capacity].set(wanted // 64)
    notes = notes.astype(jnp.bfloat16).reshape(shards * META, DM)

    base = memory[src_local]
    prepared = prepare(src_local[:, None], pending_index, base, messages, w_query)
    queries, source = make_queries(position, prepared, notes, pending, nslots)
    segment = capacity * G + META
    arrived = lax.all_to_all(
        queries.reshape(shards, segment, DM), "mem", split_axis=0, concat_axis=0, tiled=True
    )
    pairs = make_pairs(pending_index, pending, memory, w_key, w_value)
    attended = attend(arrived.reshape(shards * segment, DM), pairs, shards, nslots)
    returned = lax.all_to_all(
        attended.reshape(shards, capacity * G, DM), "mem", split_axis=0, concat_axis=0, tiled=True
    ).reshape(nslots * G, DM)

    sums = make_gates(messages, source, w_input, w_hidden)
    return updated(position, returned, sums, source, w_input)


def solution(mesh):
    placed = (
        P("mem", None),
        P(("loop", "mem"), None),
        P(("loop", "mem")),
        P(("loop", "mem")),
        P(("loop", "mem"), None),
        P(("loop", "mem"), None),
        P(("loop", "mem")),
        P(("loop", "mem")),
        P(),
        P(),
        P(),
        P(),
        P(),
    )
    return jax.shard_map(
        body, mesh=mesh, in_specs=placed, out_specs=P(("loop", "mem"), None), check_vma=False
    )
```

```python
import jax
import jax.numpy as jnp
from jax import lax
from jax.experimental import pallas as pl
from jax.experimental.pallas import tpu as pltpu
from jax.sharding import PartitionSpec as P

DM = 512
HEADS = 2
HEAD_DIM = 256
BR = 32
G = 8
SMALL = 24 * 1024 * 1024
LARGE = 48 * 1024 * 1024
SPAN = 8
MASKED = -1e30


def shifted(block, axis, distance):
    size = lax.axis_size(axis)
    route = [((i - distance) % size, i) for i in range(size)]
    return lax.ppermute(block, axis, route)


CHUNK = 512
PART = 128
TILE = 512
META = 16


def vmem_out(shape, dtype):
    return pltpu.VMEM(shape, dtype)


def hbm_out(shape, dtype):
    return pltpu.HBM(shape, dtype)


def in_hbm(array):
    return pltpu.with_memory_space_constraint(array, pltpu.HBM)


WHOLE = pl.BlockSpec(memory_space=pltpu.VMEM)
THERE = pl.BlockSpec(memory_space=pl.ANY)
SCALARS = pl.BlockSpec(memory_space=pltpu.SMEM)


def prepare_kernel(
    source_index, pending_index, base, messages, w_query, chosen, hit, held, spoken, weight
):
    held[...] = base[...]
    weight[...] = w_query[:DM, :]
    for start in range(0, base.shape[0], CHUNK):
        rows = slice(start, start + CHUNK)
        same = jnp.where(source_index[rows, :] == pending_index[...], 1.0, 0.0)
        chosen[rows, :] = same.astype(jnp.bfloat16)
        hit[rows, :] = jnp.broadcast_to(jnp.max(same, axis=1, keepdims=True), (CHUNK, 128))
        spoken[rows, :] = jnp.dot(
            messages[rows, :], w_query[DM:, :], preferred_element_type=jnp.float32
        )


def prepare(source_index, pending_index, base, messages, w_query):
    events = base.shape[0]
    return pl.pallas_call(
        prepare_kernel,
        out_shape=(
            vmem_out((events, pending_index.shape[1]), jnp.bfloat16),
            vmem_out((events, 128), jnp.float32),
            vmem_out((events, DM), jnp.bfloat16),
            vmem_out((events, DM), jnp.float32),
            vmem_out((DM, DM), jnp.bfloat16),
        ),
        in_specs=[WHOLE] * 5,
        out_specs=(WHOLE,) * 5,
        compiler_params=pltpu.CompilerParams(vmem_limit_bytes=SMALL),
        cost_estimate=pl.CostEstimate(
            flops=300_000_000, bytes_accessed=8_000_000, transcendentals=0
        ),
        name="prepare",
    )(source_index, pending_index, base, messages, w_query)


def query_kernel(
    position,
    chosen,
    hit,
    base,
    spoken,
    w_query,
    notes,
    pending,
    slots,
    source,
    arrived,
    staged,
    packed,
    kept,
    sems,
):
    load = pltpu.make_async_copy(pending, arrived, sems.at[0])
    load.start()
    events = base.shape[0]
    owners = notes.shape[0] // META
    high = staged.shape[0] // owners
    segment = high + META
    staged[...] = jnp.zeros_like(staged)
    load.wait()
    for start in range(0, events, CHUNK):
        rows = slice(start, start + CHUNK)
        picked = jnp.dot(chosen[rows, :], arrived[...], preferred_element_type=jnp.float32)
        merged = jnp.where(
            hit[rows, :1] > 0.0, picked, base[rows, :].astype(jnp.float32)
        ).astype(jnp.bfloat16)
        kept[rows, :] = merged
        found = jnp.dot(merged, w_query[...], preferred_element_type=jnp.float32) + spoken[rows, :]
        for item in range(CHUNK // G):
            place = pl.multiple_of(position[start // G + item] * G, G)
            staged[pl.ds(place, G), :] = found[item * G : (item + 1) * G, :]
    copies = []
    parts = 4
    for part in range(parts):
        for owner in range(part * owners // parts, (part + 1) * owners // parts):
            first = owner * segment
            packed[first : first + high, :] = staged[owner * high : (owner + 1) * high, :].astype(
                jnp.bfloat16
            )
            packed[first + high : first + segment, :] = notes[owner * META : (owner + 1) * META, :]
        span = owners // parts * segment
        rows = slice(part * span, (part + 1) * span)
        copies.append(
            pltpu.make_async_copy(packed.at[rows, :], slots.at[rows, :], sems.at[1 + part])
        )
        copies[-1].start()
    copies.append(pltpu.make_async_copy(kept, source, sems.at[1 + parts]))
    copies[-1].start()
    for copy in copies:
        copy.wait()


def make_queries(position, prepared, notes, pending, nslots):
    events = pending.shape[0]
    total = nslots * G + notes.shape[0]
    return pl.pallas_call(
        query_kernel,
        out_shape=(hbm_out((total, DM), jnp.bfloat16), hbm_out((events, DM), jnp.bfloat16)),
        in_specs=[SCALARS] + [WHOLE] * 6 + [THERE],
        out_specs=(THERE, THERE),
        scratch_shapes=[
            pltpu.VMEM(pending.shape, jnp.bfloat16),
            pltpu.VMEM((nslots * G, DM), jnp.float32),
            pltpu.VMEM((total, DM), jnp.bfloat16),
            pltpu.VMEM((events, DM), jnp.bfloat16),
            pltpu.SemaphoreType.DMA((6,)),
        ],
        compiler_params=pltpu.CompilerParams(vmem_limit_bytes=SMALL),
        cost_estimate=pl.CostEstimate(
            flops=2_000_000_000, bytes_accessed=8_000_000, transcendentals=0
        ),
        name="queries",
    )(position, *prepared, notes, in_hbm(pending))


def pairs_kernel(pending_index, pending, memory, w_key, w_value, *pairs):
    first = pl.program_id(0) * TILE
    row = first + lax.broadcasted_iota(jnp.int32, (TILE, 1), 0)
    chosen = jnp.where(row == pending_index[...], 1.0, 0.0)
    hit = jnp.max(chosen, axis=1, keepdims=True) > 0.0
    picked = jnp.dot(chosen.astype(jnp.bfloat16), pending[...], preferred_element_type=jnp.float32)
    merged = jnp.where(hit, picked, memory[...].astype(jnp.float32)).astype(jnp.bfloat16)
    for weight, part in ((w_key, pairs[:HEADS]), (w_value, pairs[HEADS:])):
        rows = jnp.dot(merged, weight[...], preferred_element_type=jnp.float32).astype(jnp.bfloat16)
        for head in range(HEADS):
            part[head][...] = rows[:, head * HEAD_DIM : (head + 1) * HEAD_DIM]


def make_pairs(pending_index, pending, memory, w_key, w_value):
    rows = memory.shape[0]
    whole = lambda array: pl.BlockSpec(array.shape, lambda i: (0, 0))
    return pl.pallas_call(
        pairs_kernel,
        out_shape=(jax.ShapeDtypeStruct((rows, HEAD_DIM), jnp.bfloat16),) * (2 * HEADS),
        grid=(rows // TILE,),
        in_specs=[
            whole(pending_index),
            whole(pending),
            pl.BlockSpec((TILE, DM), lambda i: (i, 0)),
            whole(w_key),
            whole(w_value),
        ],
        out_specs=(pl.BlockSpec((TILE, HEAD_DIM), lambda i: (i, 0)),) * (2 * HEADS),
        compiler_params=pltpu.CompilerParams(
            dimension_semantics=("arbitrary",), vmem_limit_bytes=LARGE
        ),
        cost_estimate=pl.CostEstimate(
            flops=17_200_000_000, bytes_accessed=28_000_000, transcendentals=0
        ),
        name="pairs",
    )(pending_index, pending, memory, w_key, w_value)


SEGMENTS = 8


def attend_kernel(
    queries, key_0, key_1, value_0, value_1, attended, weights, result, numbers, blocks, *rest
):
    pairs, sems = rest[: 2 * HEADS], rest[2 * HEADS]
    capacity = key_0.shape[0] // BR // numbers.shape[0]
    shards = numbers.shape[0]
    segment = capacity * G + META
    batches = shards // SEGMENTS
    loads = [
        pltpu.make_async_copy(there, here, sems.at[1 + number])
        for number, (there, here) in enumerate(zip((key_0, key_1, value_0, value_1), pairs))
    ]
    for copy in loads:
        copy.start()
    for part in range(shards):
        first = part * segment + capacity * G
        numbers[part : part + 1, :] = (
            queries[first : first + META, :128].astype(jnp.float32)[1:2, :].astype(jnp.int32)
        )
    copy = pltpu.make_async_copy(numbers, blocks, sems.at[0])
    copy.start()

    keys_wide = SPAN * BR
    rows_high = SPAN * G
    lane = lax.broadcasted_iota(jnp.int32, (rows_high, keys_wide), 1)
    row = lax.broadcasted_iota(jnp.int32, (rows_high, keys_wide), 0)
    own = (lane // BR) == (row // G)
    offset = lax.rem(lax.broadcasted_iota(jnp.int32, (1, keys_wide), 1), BR).astype(jnp.float32)
    groups = capacity // SPAN
    batch_groups = SEGMENTS * groups
    batch_rows = batch_groups * rows_high
    copy.wait()

    def slices(array, step, part, group):
        where = step * SEGMENTS + part
        return jnp.concatenate(
            [
                array[pl.ds(pl.multiple_of(blocks[where, group * SPAN + item] * BR, BR), BR), :]
                for item in range(SPAN)
            ],
            0,
        )

    for head in range(HEADS):
        columns = slice(head * HEAD_DIM, (head + 1) * HEAD_DIM)
        loads[head].wait()

        @pl.loop(0, batches)
        def _(step):
            scores = []
            for part in range(SEGMENTS):
                top = pl.multiple_of((step * SEGMENTS + part) * segment, META)
                told = queries[pl.ds(top + capacity * G, META), :].astype(jnp.float32)
                for group in range(groups):
                    length = told[0:1, group * keys_wide : (group + 1) * keys_wide]
                    usable = own & (offset < length)
                    query = queries[pl.ds(top + group * rows_high, rows_high), columns]
                    score = lax.dot_general(
                        query,
                        slices(pairs[head], step, part, group),
                        (((1,), (1,)), ((), ())),
                        preferred_element_type=jnp.float32,
                    ) * (1.0 / 16.0)
                    scores.append(jnp.where(usable, score, MASKED))
            scores = jnp.concatenate(scores, 0)
            expons = jnp.exp(scores - jnp.max(scores, axis=1, keepdims=True))
            first = pl.multiple_of(step * batch_rows, batch_rows)
            weights[head, pl.ds(first, batch_rows), :] = (
                expons * (1.0 / jnp.sum(expons, axis=1, keepdims=True))
            ).astype(jnp.bfloat16)

    for head in range(HEADS):
        columns = slice(head * HEAD_DIM, (head + 1) * HEAD_DIM)
        loads[HEADS + head].wait()

        @pl.loop(0, batches)
        def _(step):
            for part in range(SEGMENTS):
                for group in range(groups):
                    place = step * batch_rows + (part * groups + group) * rows_high
                    rows = pl.ds(pl.multiple_of(place, rows_high), rows_high)
                    result[rows, columns] = jnp.dot(
                        weights[head, rows, :],
                        slices(pairs[HEADS + head], step, part, group),
                        preferred_element_type=jnp.float32,
                    ).astype(jnp.bfloat16)
            if head == HEADS - 1:
                done = pl.ds(pl.multiple_of(step * batch_rows, batch_rows), batch_rows)
                pltpu.make_async_copy(result.at[done, :], attended.at[done, :], sems.at[0]).start()

    pltpu.make_async_copy(result, attended, sems.at[0]).wait()


def attend(queries, pairs, shards, nslots):
    return pl.pallas_call(
        attend_kernel,
        out_shape=hbm_out((nslots * G, DM), jnp.bfloat16),
        in_specs=[WHOLE] + [THERE] * (2 * HEADS),
        out_specs=THERE,
        scratch_shapes=[
            pltpu.VMEM((HEADS, nslots * G, SPAN * BR), jnp.bfloat16),
            pltpu.VMEM((nslots * G, DM), jnp.bfloat16),
            pltpu.VMEM((shards, 128), jnp.int32),
            pltpu.SMEM((shards, 128), jnp.int32),
        ]
        + [pltpu.VMEM(array.shape, jnp.bfloat16) for array in pairs]
        + [pltpu.SemaphoreType.DMA((1 + 2 * HEADS,))],
        compiler_params=pltpu.CompilerParams(vmem_limit_bytes=LARGE),
        cost_estimate=pl.CostEstimate(
            flops=4_000_000_000, bytes_accessed=20_000_000, transcendentals=1_000_000
        ),
        name="attend",
    )(queries, *[in_hbm(array) for array in pairs])


def gate_kernel(messages, source, w_input, w_hidden, sums):
    msg = messages.shape[1]
    spoken = jnp.dot(messages[...], w_input[:msg, :], preferred_element_type=jnp.float32)
    hidden = jnp.dot(source[...], w_hidden[...], preferred_element_type=jnp.float32)
    sums[:, : 2 * DM] = spoken[:, : 2 * DM] + hidden[:, : 2 * DM]
    sums[:, 2 * DM : 3 * DM] = spoken[:, 2 * DM :]
    sums[:, 3 * DM :] = hidden[:, 2 * DM :]


def make_gates(messages, source, w_input, w_hidden):
    events, msg = messages.shape
    high = 256
    whole = lambda array: pl.BlockSpec(array.shape, lambda i: (0, 0))
    part = lambda wide: pl.BlockSpec((high, wide), lambda i: (i, 0))
    return pl.pallas_call(
        gate_kernel,
        out_shape=jax.ShapeDtypeStruct((events, 4 * DM), jnp.float32),
        grid=(events // high,),
        in_specs=[part(msg), part(DM), whole(w_input), whole(w_hidden)],
        out_specs=part(4 * DM),
        compiler_params=pltpu.CompilerParams(
            dimension_semantics=("arbitrary",), vmem_limit_bytes=LARGE
        ),
        cost_estimate=pl.CostEstimate(
            flops=2_400_000_000, bytes_accessed=15_000_000, transcendentals=0
        ),
        name="gates",
    )(messages, source, w_input, w_hidden)


LOADED = 256


def update_kernel(
    position,
    returned,
    sums,
    source,
    w_input,
    fresh,
    sums_here,
    source_here,
    weight,
    ordered,
    result,
    sems,
):
    events = source.shape[0]
    base = w_input.shape[0] - weight.shape[0]
    pieces = events // LOADED
    first_loads = [
        pltpu.make_async_copy(w_input.at[base:, :], weight, sems.at[0]),
        pltpu.make_async_copy(source, source_here, sems.at[1]),
    ]
    loads = []
    for piece in range(pieces):
        rows = slice(piece * LOADED, (piece + 1) * LOADED)
        loads.append(
            pltpu.make_async_copy(sums.at[rows, :], sums_here.at[rows, :], sems.at[2 + piece])
        )
    for copy in first_loads[:1] + loads[:1] + first_loads[1:] + loads[1:]:
        copy.start()
    copies = []
    for number in range(events // PART):
        rows = slice(number * PART, (number + 1) * PART)
        for item in range(PART // G):
            place = position[number * (PART // G) + item]
            couple = pl.multiple_of((place // 2) * 2 * G, 2 * G)
            pair = returned[pl.ds(couple, 2 * G), :].astype(jnp.float32)
            top = number * PART + item * G
            ordered[top : top + G, :] = jnp.where(
                lax.rem(place, 2) == 0, pair[:G, :], pair[G:, :]
            )
        if number == 0:
            first_loads[0].wait()
        attended = ordered[rows, :].astype(jnp.bfloat16)
        gates = jnp.dot(attended, weight[...], preferred_element_type=jnp.float32)
        if number * PART % LOADED == 0:
            loads[number * PART // LOADED].wait()
        if number == 0:
            first_loads[1].wait()
        reset = jax.nn.sigmoid(gates[:, :DM] + sums_here[rows, :DM])
        update = jax.nn.sigmoid(gates[:, DM : 2 * DM] + sums_here[rows, DM : 2 * DM])
        candidate = jnp.tanh(
            gates[:, 2 * DM :] + sums_here[rows, 2 * DM : 3 * DM] + reset * sums_here[rows, 3 * DM :]
        )
        result[rows, :] = (
            (1.0 - update) * candidate + update * source_here[rows, :].astype(jnp.float32)
        ).astype(jnp.bfloat16)
        copies.append(
            pltpu.make_async_copy(
                result.at[rows, :], fresh.at[rows, :], sems.at[2 + pieces + number]
            )
        )
        copies[-1].start()
    for copy in copies:
        copy.wait()


def updated(position, returned, sums, source, w_input):
    events = source.shape[0]
    return pl.pallas_call(
        update_kernel,
        out_shape=hbm_out((events, DM), jnp.bfloat16),
        in_specs=[SCALARS, WHOLE] + [THERE] * 3,
        out_specs=THERE,
        scratch_shapes=[
            pltpu.VMEM(sums.shape, jnp.float32),
            pltpu.VMEM(source.shape, jnp.bfloat16),
            pltpu.VMEM((DM, 3 * DM), jnp.bfloat16),
            pltpu.VMEM((events, DM), jnp.float32),
            pltpu.VMEM((events, DM), jnp.bfloat16),
            pltpu.SemaphoreType.DMA((2 + events // LOADED + events // PART,)),
        ],
        compiler_params=pltpu.CompilerParams(vmem_limit_bytes=LARGE),
        cost_estimate=pl.CostEstimate(
            flops=1_700_000_000, bytes_accessed=15_000_000, transcendentals=1_500_000
        ),
        name="update",
    )(position, returned, *[in_hbm(array) for array in (sums, source, w_input)])


def body(
    memory,
    sectioned_rows,
    sectioned_index,
    src_local,
    messages,
    block_owner,
    block_local,
    block_len,
    w_query,
    w_key,
    w_value,
    w_input,
    w_hidden,
):
    shards = lax.axis_size("mem")
    nblocks = block_local.shape[0]
    capacity = max(2, 2 * nblocks // shards)
    nslots = shards * capacity

    pending_index = shifted(sectioned_index, "loop", 1)[None, :]
    pending = shifted(sectioned_rows, "loop", 1)

    owners = block_owner[:, 0]
    onehot = (owners[:, None] == jnp.arange(shards, dtype=jnp.int32)[None, :]).astype(jnp.int32)
    rank = jnp.sum((jnp.cumsum(onehot, 0) - onehot) * onehot, 1)
    position = owners * capacity + rank
    unused = (lax.axis_index("mem") * capacity + jnp.arange(nslots, dtype=jnp.int32) % capacity) * 64
    wanted = unused.at[position].set(block_local * 64 + block_len)
    wanted = wanted.reshape(shards, capacity)
    notes = jnp.zeros((shards, META, DM), jnp.int32)
    notes = notes.at[:, 0, : capacity * BR].set(jnp.repeat(wanted % 64, BR, axis=1))
    notes = notes.at[:, 1, :capacity].set(wanted // 64)
    notes = notes.astype(jnp.bfloat16).reshape(shards * META, DM)

    base = memory[src_local]
    prepared = prepare(src_local[:, None], pending_index, base, messages, w_query)
    queries, source = make_queries(position, prepared, notes, pending, nslots)
    segment = capacity * G + META
    arrived = lax.all_to_all(
        queries.reshape(shards, segment, DM), "mem", split_axis=0, concat_axis=0, tiled=True
    )
    pairs = make_pairs(pending_index, pending, memory, w_key, w_value)
    attended = attend(arrived.reshape(shards * segment, DM), pairs, shards, nslots)
    returned = lax.all_to_all(
        attended.reshape(shards, capacity * G, DM), "mem", split_axis=0, concat_axis=0, tiled=True
    ).reshape(nslots * G, DM)

    sums = make_gates(messages, source, w_input, w_hidden)
    return updated(position, returned, sums, source, w_input)


def solution(mesh):
    placed = (
        P("mem", None),
        P(("loop", "mem"), None),
        P(("loop", "mem")),
        P(("loop", "mem")),
        P(("loop", "mem"), None),
        P(("loop", "mem"), None),
        P(("loop", "mem")),
        P(("loop", "mem")),
        P(),
        P(),
        P(),
        P(),
        P(),
    )
    return jax.shard_map(
        body, mesh=mesh, in_specs=placed, out_specs=P(("loop", "mem"), None), check_vma=False
    )
```

```python
import jax
import jax.numpy as jnp
from jax import lax
from jax.experimental import pallas as pl
from jax.experimental.pallas import tpu as pltpu
from jax.sharding import PartitionSpec as P

DM = 512
HEADS = 2
HEAD_DIM = 256
BR = 32
G = 8
SMALL = 24 * 1024 * 1024
LARGE = 48 * 1024 * 1024
SPAN = 8
MASKED = -1e30


def shifted(block, axis, distance):
    size = lax.axis_size(axis)
    route = [((i - distance) % size, i) for i in range(size)]
    return lax.ppermute(block, axis, route)


CHUNK = 512
PART = 128
TILE = 512
META = 8


def vmem_out(shape, dtype):
    return pltpu.VMEM(shape, dtype)


def hbm_out(shape, dtype):
    return pltpu.HBM(shape, dtype)


def in_hbm(array):
    return pltpu.with_memory_space_constraint(array, pltpu.HBM)


WHOLE = pl.BlockSpec(memory_space=pltpu.VMEM)
THERE = pl.BlockSpec(memory_space=pl.ANY)
SCALARS = pl.BlockSpec(memory_space=pltpu.SMEM)


def prepare_kernel(
    source_index, pending_index, base, messages, w_query, chosen, hit, held, spoken, weight
):
    held[...] = base[...]
    weight[...] = w_query[:DM, :]
    for start in range(0, base.shape[0], CHUNK):
        rows = slice(start, start + CHUNK)
        same = jnp.where(source_index[rows, :] == pending_index[...], 1.0, 0.0)
        chosen[rows, :] = same.astype(jnp.bfloat16)
        hit[rows, :] = jnp.broadcast_to(jnp.max(same, axis=1, keepdims=True), (CHUNK, 128))
        spoken[rows, :] = jnp.dot(
            messages[rows, :], w_query[DM:, :], preferred_element_type=jnp.float32
        )


def prepare(source_index, pending_index, base, messages, w_query):
    events = base.shape[0]
    return pl.pallas_call(
        prepare_kernel,
        out_shape=(
            vmem_out((events, pending_index.shape[1]), jnp.bfloat16),
            vmem_out((events, 128), jnp.float32),
            vmem_out((events, DM), jnp.bfloat16),
            vmem_out((events, DM), jnp.float32),
            vmem_out((DM, DM), jnp.bfloat16),
        ),
        in_specs=[WHOLE] * 5,
        out_specs=(WHOLE,) * 5,
        compiler_params=pltpu.CompilerParams(vmem_limit_bytes=SMALL),
        cost_estimate=pl.CostEstimate(
            flops=300_000_000, bytes_accessed=8_000_000, transcendentals=0
        ),
        name="prepare",
    )(source_index, pending_index, base, messages, w_query)


def query_kernel(
    position,
    chosen,
    hit,
    base,
    spoken,
    w_query,
    notes,
    pending,
    slots,
    source,
    staged,
    packed,
    kept,
    sems,
):
    events = base.shape[0]
    owners = notes.shape[0] // META
    high = staged.shape[0] // owners
    segment = high + META
    staged[...] = jnp.zeros_like(staged)
    for start in range(0, events, CHUNK):
        rows = slice(start, start + CHUNK)
        picked = jnp.dot(chosen[rows, :], pending[...], preferred_element_type=jnp.float32)
        merged = jnp.where(
            hit[rows, :1] > 0.0, picked, base[rows, :].astype(jnp.float32)
        ).astype(jnp.bfloat16)
        kept[rows, :] = merged
        found = jnp.dot(merged, w_query[...], preferred_element_type=jnp.float32) + spoken[rows, :]
        for item in range(CHUNK // G):
            place = pl.multiple_of(position[start // G + item] * G, G)
            staged[pl.ds(place, G), :] = found[item * G : (item + 1) * G, :]
    copies = []
    parts = 4
    for part in range(parts):
        for owner in range(part * owners // parts, (part + 1) * owners // parts, 2):
            couple = [
                piece
                for each in (owner, owner + 1)
                for piece in (
                    staged[each * high : (each + 1) * high, :],
                    notes[each * META : (each + 1) * META, :],
                )
            ]
            packed[owner * segment : (owner + 2) * segment, :] = jnp.concatenate(couple, 0).astype(
                jnp.bfloat16
            )
        span = owners // parts * segment
        rows = slice(part * span, (part + 1) * span)
        copies.append(
            pltpu.make_async_copy(packed.at[rows, :], slots.at[rows, :], sems.at[part])
        )
        copies[-1].start()
    copies.append(pltpu.make_async_copy(kept, source, sems.at[parts]))
    copies[-1].start()
    for copy in copies:
        copy.wait()


def make_queries(position, prepared, notes, pending, nslots):
    events = pending.shape[0]
    total = nslots * G + notes.shape[0]
    return pl.pallas_call(
        query_kernel,
        out_shape=(hbm_out((total, DM), jnp.bfloat16), hbm_out((events, DM), jnp.bfloat16)),
        in_specs=[SCALARS] + [WHOLE] * 7,
        out_specs=(THERE, THERE),
        scratch_shapes=[
            pltpu.VMEM((nslots * G, DM), jnp.float32),
            pltpu.VMEM((total, DM), jnp.bfloat16),
            pltpu.VMEM((events, DM), jnp.bfloat16),
            pltpu.SemaphoreType.DMA((5,)),
        ],
        compiler_params=pltpu.CompilerParams(vmem_limit_bytes=SMALL),
        cost_estimate=pl.CostEstimate(
            flops=2_000_000_000, bytes_accessed=8_000_000, transcendentals=0
        ),
        name="queries",
    )(position, *prepared, notes, pending)


def pairs_kernel(pending_index, pending, memory, w_key, w_value, *pairs):
    first = pl.program_id(0) * TILE
    row = first + lax.broadcasted_iota(jnp.int32, (TILE, 1), 0)
    chosen = jnp.where(row == pending_index[...], 1.0, 0.0)
    hit = jnp.max(chosen, axis=1, keepdims=True) > 0.0
    picked = jnp.dot(chosen.astype(jnp.bfloat16), pending[...], preferred_element_type=jnp.float32)
    merged = jnp.where(hit, picked, memory[...].astype(jnp.float32)).astype(jnp.bfloat16)
    for weight, part in ((w_key, pairs[:HEADS]), (w_value, pairs[HEADS:])):
        rows = jnp.dot(merged, weight[...], preferred_element_type=jnp.float32).astype(jnp.bfloat16)
        for head in range(HEADS):
            part[head][...] = rows[:, head * HEAD_DIM : (head + 1) * HEAD_DIM]


def make_pairs(pending_index, pending, memory, w_key, w_value):
    rows = memory.shape[0]
    whole = lambda array: pl.BlockSpec(array.shape, lambda i: (0, 0))
    return pl.pallas_call(
        pairs_kernel,
        out_shape=(jax.ShapeDtypeStruct((rows, HEAD_DIM), jnp.bfloat16),) * (2 * HEADS),
        grid=(rows // TILE,),
        in_specs=[
            whole(pending_index),
            WHOLE,
            pl.BlockSpec((TILE, DM), lambda i: (i, 0)),
            whole(w_key),
            whole(w_value),
        ],
        out_specs=(pl.BlockSpec((TILE, HEAD_DIM), lambda i: (i, 0)),) * (2 * HEADS),
        compiler_params=pltpu.CompilerParams(
            dimension_semantics=("arbitrary",), vmem_limit_bytes=LARGE
        ),
        cost_estimate=pl.CostEstimate(
            flops=17_200_000_000, bytes_accessed=28_000_000, transcendentals=0
        ),
        name="pairs",
    )(pending_index, pending, memory, w_key, w_value)


SEGMENTS = 8


def attend_kernel(
    queries, key_0, key_1, value_0, value_1, attended, weights, result, numbers, blocks, *rest
):
    pairs, sems = rest[: 2 * HEADS], rest[2 * HEADS]
    capacity = key_0.shape[0] // BR // numbers.shape[0]
    shards = numbers.shape[0]
    segment = capacity * G + META
    batches = shards // SEGMENTS
    loads = [
        pltpu.make_async_copy(there, here, sems.at[1 + number])
        for number, (there, here) in enumerate(zip((key_0, key_1, value_0, value_1), pairs))
    ]
    for copy in loads:
        copy.start()
    for part in range(shards):
        first = part * segment + capacity * G - META * (part % 2)
        notes = queries[first : first + 2 * META, :128].astype(jnp.float32)
        mark = META * (part % 2) + 1
        numbers[part : part + 1, :] = notes[mark : mark + 1, :].astype(jnp.int32)
    copy = pltpu.make_async_copy(numbers, blocks, sems.at[0])
    copy.start()

    keys_wide = SPAN * BR
    rows_high = SPAN * G
    lane = lax.broadcasted_iota(jnp.int32, (rows_high, keys_wide), 1)
    row = lax.broadcasted_iota(jnp.int32, (rows_high, keys_wide), 0)
    own = (lane // BR) == (row // G)
    offset = lax.rem(lax.broadcasted_iota(jnp.int32, (1, keys_wide), 1), BR).astype(jnp.float32)
    groups = capacity // SPAN
    batch_groups = SEGMENTS * groups
    batch_rows = batch_groups * rows_high
    copy.wait()

    def slices(array, step, part, group):
        where = step * SEGMENTS + part
        return jnp.concatenate(
            [
                array[pl.ds(pl.multiple_of(blocks[where, group * SPAN + item] * BR, BR), BR), :]
                for item in range(SPAN)
            ],
            0,
        )

    for head in range(HEADS):
        columns = slice(head * HEAD_DIM, (head + 1) * HEAD_DIM)
        loads[head].wait()

        @pl.loop(0, batches)
        def _(step):
            scores = []
            for part in range(SEGMENTS):
                shift = META * (part % 2)
                top = pl.multiple_of((step * SEGMENTS + part) * segment - shift, 2 * META)
                told = queries[pl.ds(top + capacity * G, 2 * META), :].astype(jnp.float32)
                told = told[shift : shift + 1, :]
                for group in range(groups):
                    length = told[0:1, group * keys_wide : (group + 1) * keys_wide]
                    usable = own & (offset < length)
                    query = queries[pl.ds(top + group * rows_high, rows_high + 2 * shift), columns]
                    if shift:
                        query = query.astype(jnp.float32)[shift : shift + rows_high]
                        query = query.astype(jnp.bfloat16)
                    score = lax.dot_general(
                        query,
                        slices(pairs[head], step, part, group),
                        (((1,), (1,)), ((), ())),
                        preferred_element_type=jnp.float32,
                    ) * (1.0 / 16.0)
                    scores.append(jnp.where(usable, score, MASKED))
            scores = jnp.concatenate(scores, 0)
            expons = jnp.exp(scores - jnp.max(scores, axis=1, keepdims=True))
            first = pl.multiple_of(step * batch_rows, batch_rows)
            weights[head, pl.ds(first, batch_rows), :] = (
                expons * (1.0 / jnp.sum(expons, axis=1, keepdims=True))
            ).astype(jnp.bfloat16)

    for head in range(HEADS):
        columns = slice(head * HEAD_DIM, (head + 1) * HEAD_DIM)
        loads[HEADS + head].wait()

        @pl.loop(0, batches)
        def _(step):
            for part in range(SEGMENTS):
                for group in range(groups):
                    place = step * batch_rows + (part * groups + group) * rows_high
                    rows = pl.ds(pl.multiple_of(place, rows_high), rows_high)
                    result[rows, columns] = jnp.dot(
                        weights[head, rows, :],
                        slices(pairs[HEADS + head], step, part, group),
                        preferred_element_type=jnp.float32,
                    ).astype(jnp.bfloat16)
            if head == HEADS - 1:
                done = pl.ds(pl.multiple_of(step * batch_rows, batch_rows), batch_rows)
                pltpu.make_async_copy(result.at[done, :], attended.at[done, :], sems.at[0]).start()

    pltpu.make_async_copy(result, attended, sems.at[0]).wait()


def attend(queries, pairs, shards, nslots):
    return pl.pallas_call(
        attend_kernel,
        out_shape=hbm_out((nslots * G, DM), jnp.bfloat16),
        in_specs=[WHOLE] + [THERE] * (2 * HEADS),
        out_specs=THERE,
        scratch_shapes=[
            pltpu.VMEM((HEADS, nslots * G, SPAN * BR), jnp.bfloat16),
            pltpu.VMEM((nslots * G, DM), jnp.bfloat16),
            pltpu.VMEM((shards, 128), jnp.int32),
            pltpu.SMEM((shards, 128), jnp.int32),
        ]
        + [pltpu.VMEM(array.shape, jnp.bfloat16) for array in pairs]
        + [pltpu.SemaphoreType.DMA((1 + 2 * HEADS,))],
        compiler_params=pltpu.CompilerParams(vmem_limit_bytes=LARGE),
        cost_estimate=pl.CostEstimate(
            flops=4_000_000_000, bytes_accessed=20_000_000, transcendentals=1_000_000
        ),
        name="attend",
    )(queries, *[in_hbm(array) for array in pairs])


def gate_kernel(messages, source, w_input, w_hidden, sums):
    msg = messages.shape[1]
    spoken = jnp.dot(messages[...], w_input[:msg, :], preferred_element_type=jnp.float32)
    hidden = jnp.dot(source[...], w_hidden[...], preferred_element_type=jnp.float32)
    sums[:, : 2 * DM] = spoken[:, : 2 * DM] + hidden[:, : 2 * DM]
    sums[:, 2 * DM : 3 * DM] = spoken[:, 2 * DM :]
    sums[:, 3 * DM :] = hidden[:, 2 * DM :]


def make_gates(messages, source, w_input, w_hidden):
    events, msg = messages.shape
    high = 256
    whole = lambda array: pl.BlockSpec(array.shape, lambda i: (0, 0))
    part = lambda wide: pl.BlockSpec((high, wide), lambda i: (i, 0))
    return pl.pallas_call(
        gate_kernel,
        out_shape=jax.ShapeDtypeStruct((events, 4 * DM), jnp.float32),
        grid=(events // high,),
        in_specs=[part(msg), part(DM), whole(w_input), whole(w_hidden)],
        out_specs=part(4 * DM),
        compiler_params=pltpu.CompilerParams(
            dimension_semantics=("arbitrary",), vmem_limit_bytes=LARGE
        ),
        cost_estimate=pl.CostEstimate(
            flops=2_400_000_000, bytes_accessed=15_000_000, transcendentals=0
        ),
        name="gates",
    )(messages, source, w_input, w_hidden)


LOADED = 256


def update_kernel(
    position,
    returned,
    sums,
    source,
    w_input,
    fresh,
    sums_here,
    source_here,
    weight,
    ordered,
    result,
    sems,
):
    events = source.shape[0]
    base = w_input.shape[0] - weight.shape[0]
    edges = [0, PART, 2 * PART] + list(range(2 * PART + LOADED, events + 1, LOADED))
    loads = {}
    pieces = 0
    for low, top in zip(edges[:-1], edges[1:]):
        rows = slice(low, top)
        loads[low] = [
            pltpu.make_async_copy(there.at[rows, :], here.at[rows, :], sems.at[1 + pieces + kind])
            for kind, (there, here) in enumerate(((sums, sums_here), (source, source_here)))
        ]
        pieces += 2
    first_load = pltpu.make_async_copy(w_input.at[base:, :], weight, sems.at[0])
    first_load.start()
    for low in edges[:-1]:
        for copy in loads[low]:
            copy.start()
    copies = []
    for number in range(events // PART):
        rows = slice(number * PART, (number + 1) * PART)
        for item in range(PART // G):
            place = position[number * (PART // G) + item]
            couple = pl.multiple_of((place // 2) * 2 * G, 2 * G)
            pair = returned[pl.ds(couple, 2 * G), :].astype(jnp.float32)
            top = number * PART + item * G
            ordered[top : top + G, :] = jnp.where(
                lax.rem(place, 2) == 0, pair[:G, :], pair[G:, :]
            )
        if number == 0:
            first_load.wait()
        attended = ordered[rows, :].astype(jnp.bfloat16)
        gates = jnp.dot(attended, weight[...], preferred_element_type=jnp.float32)
        for copy in loads.get(number * PART, []):
            copy.wait()
        reset = jax.nn.sigmoid(gates[:, :DM] + sums_here[rows, :DM])
        update = jax.nn.sigmoid(gates[:, DM : 2 * DM] + sums_here[rows, DM : 2 * DM])
        candidate = jnp.tanh(
            gates[:, 2 * DM :] + sums_here[rows, 2 * DM : 3 * DM] + reset * sums_here[rows, 3 * DM :]
        )
        result[rows, :] = (
            (1.0 - update) * candidate + update * source_here[rows, :].astype(jnp.float32)
        ).astype(jnp.bfloat16)
        copies.append(
            pltpu.make_async_copy(
                result.at[rows, :], fresh.at[rows, :], sems.at[1 + pieces + number]
            )
        )
        copies[-1].start()
    for copy in copies:
        copy.wait()


def updated(position, returned, sums, source, w_input):
    events = source.shape[0]
    return pl.pallas_call(
        update_kernel,
        out_shape=hbm_out((events, DM), jnp.bfloat16),
        in_specs=[SCALARS, WHOLE] + [THERE] * 3,
        out_specs=THERE,
        scratch_shapes=[
            pltpu.VMEM(sums.shape, jnp.float32),
            pltpu.VMEM(source.shape, jnp.bfloat16),
            pltpu.VMEM((DM, 3 * DM), jnp.bfloat16),
            pltpu.VMEM((events, DM), jnp.float32),
            pltpu.VMEM((events, DM), jnp.bfloat16),
            pltpu.SemaphoreType.DMA((3 + 2 * (events // LOADED) + events // PART,)),
        ],
        compiler_params=pltpu.CompilerParams(vmem_limit_bytes=LARGE),
        cost_estimate=pl.CostEstimate(
            flops=1_700_000_000, bytes_accessed=15_000_000, transcendentals=1_500_000
        ),
        name="update",
    )(position, returned, *[in_hbm(array) for array in (sums, source, w_input)])


def body(
    memory,
    sectioned_rows,
    sectioned_index,
    src_local,
    messages,
    block_owner,
    block_local,
    block_len,
    w_query,
    w_key,
    w_value,
    w_input,
    w_hidden,
):
    shards = lax.axis_size("mem")
    nblocks = block_local.shape[0]
    capacity = max(2, 2 * nblocks // shards)
    nslots = shards * capacity

    pending_index = shifted(sectioned_index, "loop", 1)[None, :]
    pending = shifted(sectioned_rows, "loop", 1)

    owners = block_owner[:, 0]
    onehot = (owners[:, None] == jnp.arange(shards, dtype=jnp.int32)[None, :]).astype(jnp.int32)
    rank = jnp.sum((jnp.cumsum(onehot, 0) - onehot) * onehot, 1)
    position = owners * capacity + rank
    unused = (lax.axis_index("mem") * capacity + jnp.arange(nslots, dtype=jnp.int32) % capacity) * 64
    wanted = unused.at[position].set(block_local * 64 + block_len)
    wanted = wanted.reshape(shards, capacity)
    notes = jnp.zeros((shards, META, DM), jnp.int32)
    notes = notes.at[:, 0, : capacity * BR].set(jnp.repeat(wanted % 64, BR, axis=1))
    notes = notes.at[:, 1, :capacity].set(wanted // 64)
    notes = notes.astype(jnp.float32).reshape(shards * META, DM)

    base = memory[src_local]
    prepared = prepare(src_local[:, None], pending_index, base, messages, w_query)
    queries, source = make_queries(position, prepared, notes, pending, nslots)
    segment = capacity * G + META
    arrived = lax.all_to_all(
        queries.reshape(shards, segment, DM), "mem", split_axis=0, concat_axis=0, tiled=True
    )
    pairs = make_pairs(pending_index, pending, memory, w_key, w_value)
    attended = attend(arrived.reshape(shards * segment, DM), pairs, shards, nslots)
    returned = lax.all_to_all(
        attended.reshape(shards, capacity * G, DM), "mem", split_axis=0, concat_axis=0, tiled=True
    ).reshape(nslots * G, DM)

    sums = make_gates(messages, source, w_input, w_hidden)
    return updated(position, returned, sums, source, w_input)


def solution(mesh):
    placed = (
        P("mem", None),
        P(("loop", "mem"), None),
        P(("loop", "mem")),
        P(("loop", "mem")),
        P(("loop", "mem"), None),
        P(("loop", "mem"), None),
        P(("loop", "mem")),
        P(("loop", "mem")),
        P(),
        P(),
        P(),
        P(),
        P(),
    )
    return jax.shard_map(
        body, mesh=mesh, in_specs=placed, out_specs=P(("loop", "mem"), None), check_vma=False
    )
```

```python
import jax
import jax.numpy as jnp
from jax import lax
from jax.experimental import pallas as pl
from jax.experimental.pallas import tpu as pltpu
from jax.sharding import PartitionSpec as P

DM = 512
HEADS = 2
HEAD_DIM = 256
BR = 32
G = 8
SMALL = 24 * 1024 * 1024
LARGE = 48 * 1024 * 1024
SPAN = 8
MASKED = -1e30


def shifted(block, axis, distance):
    size = lax.axis_size(axis)
    route = [((i - distance) % size, i) for i in range(size)]
    return lax.ppermute(block, axis, route)


CHUNK = 512
PART = 128
TILE = 512
META = 8


def vmem_out(shape, dtype):
    return pltpu.VMEM(shape, dtype)


def hbm_out(shape, dtype):
    return pltpu.HBM(shape, dtype)


def in_hbm(array):
    return pltpu.with_memory_space_constraint(array, pltpu.HBM)


WHOLE = pl.BlockSpec(memory_space=pltpu.VMEM)
THERE = pl.BlockSpec(memory_space=pl.ANY)
SCALARS = pl.BlockSpec(memory_space=pltpu.SMEM)


def prepare_kernel(
    source_index, pending_index, base, messages, w_query, chosen, hit, held, spoken, weight
):
    held[...] = base[...]
    weight[...] = w_query[:DM, :]
    for start in range(0, base.shape[0], CHUNK):
        rows = slice(start, start + CHUNK)
        same = jnp.where(source_index[rows, :] == pending_index[...], 1.0, 0.0)
        chosen[rows, :] = same.astype(jnp.bfloat16)
        hit[rows, :] = jnp.broadcast_to(jnp.max(same, axis=1, keepdims=True), (CHUNK, 128))
        spoken[rows, :] = jnp.dot(
            messages[rows, :], w_query[DM:, :], preferred_element_type=jnp.float32
        )


def prepare(source_index, pending_index, base, messages, w_query):
    events = base.shape[0]
    return pl.pallas_call(
        prepare_kernel,
        out_shape=(
            vmem_out((events, pending_index.shape[1]), jnp.bfloat16),
            vmem_out((events, 128), jnp.float32),
            vmem_out((events, DM), jnp.bfloat16),
            vmem_out((events, DM), jnp.float32),
            vmem_out((DM, DM), jnp.bfloat16),
        ),
        in_specs=[WHOLE] * 5,
        out_specs=(WHOLE,) * 5,
        compiler_params=pltpu.CompilerParams(vmem_limit_bytes=SMALL),
        cost_estimate=pl.CostEstimate(
            flops=300_000_000, bytes_accessed=8_000_000, transcendentals=0
        ),
        name="prepare",
    )(source_index, pending_index, base, messages, w_query)


def query_kernel(
    position,
    chosen,
    hit,
    base,
    spoken,
    w_query,
    notes,
    pending,
    slots,
    source,
    staged,
    packed,
    kept,
    sems,
):
    events = base.shape[0]
    owners = notes.shape[0] // META
    high = staged.shape[0] // owners
    segment = high + META
    copies = []
    for start in range(0, events, CHUNK):
        rows = slice(start, start + CHUNK)
        picked = jnp.dot(chosen[rows, :], pending[...], preferred_element_type=jnp.float32)
        merged = jnp.where(
            hit[rows, :1] > 0.0, picked, base[rows, :].astype(jnp.float32)
        ).astype(jnp.bfloat16)
        kept[rows, :] = merged
        found = jnp.dot(merged, w_query[...], preferred_element_type=jnp.float32) + spoken[rows, :]
        for item in range(CHUNK // G):
            place = pl.multiple_of(position[start // G + item] * G, G)
            staged[pl.ds(place, G), :] = found[item * G : (item + 1) * G, :]
        copies.append(
            pltpu.make_async_copy(kept.at[rows, :], source.at[rows, :], sems.at[start // CHUNK])
        )
        copies[-1].start()
    others = len(copies)
    parts = 8
    for part in range(parts):
        for owner in range(part * owners // parts, (part + 1) * owners // parts, 2):
            couple = [
                piece
                for each in (owner, owner + 1)
                for piece in (
                    staged[each * high : (each + 1) * high, :],
                    notes[each * META : (each + 1) * META, :],
                )
            ]
            packed[owner * segment : (owner + 2) * segment, :] = jnp.concatenate(couple, 0).astype(
                jnp.bfloat16
            )
        span = owners // parts * segment
        rows = slice(part * span, (part + 1) * span)
        copies.append(
            pltpu.make_async_copy(packed.at[rows, :], slots.at[rows, :], sems.at[others + part])
        )
        copies[-1].start()
    for copy in copies:
        copy.wait()


def make_queries(position, prepared, notes, pending, nslots):
    events = pending.shape[0]
    total = nslots * G + notes.shape[0]
    return pl.pallas_call(
        query_kernel,
        out_shape=(hbm_out((total, DM), jnp.bfloat16), hbm_out((events, DM), jnp.bfloat16)),
        in_specs=[SCALARS] + [WHOLE] * 7,
        out_specs=(THERE, THERE),
        scratch_shapes=[
            pltpu.VMEM((nslots * G, DM), jnp.float32),
            pltpu.VMEM((total, DM), jnp.bfloat16),
            pltpu.VMEM((events, DM), jnp.bfloat16),
            pltpu.SemaphoreType.DMA((8 + events // CHUNK,)),
        ],
        compiler_params=pltpu.CompilerParams(vmem_limit_bytes=SMALL),
        cost_estimate=pl.CostEstimate(
            flops=2_000_000_000, bytes_accessed=8_000_000, transcendentals=0
        ),
        name="queries",
    )(position, *prepared, notes, pending)


def pairs_kernel(pending_index, pending, memory, w_key, w_value, *pairs):
    first = pl.program_id(0) * TILE
    row = first + lax.broadcasted_iota(jnp.int32, (TILE, 1), 0)
    chosen = jnp.where(row == pending_index[...], 1.0, 0.0)
    hit = jnp.max(chosen, axis=1, keepdims=True) > 0.0
    picked = jnp.dot(chosen.astype(jnp.bfloat16), pending[...], preferred_element_type=jnp.float32)
    merged = jnp.where(hit, picked, memory[...].astype(jnp.float32)).astype(jnp.bfloat16)
    for weight, part in ((w_key, pairs[:HEADS]), (w_value, pairs[HEADS:])):
        rows = jnp.dot(merged, weight[...], preferred_element_type=jnp.float32).astype(jnp.bfloat16)
        for head in range(HEADS):
            part[head][...] = rows[:, head * HEAD_DIM : (head + 1) * HEAD_DIM]


def make_pairs(pending_index, pending, memory, w_key, w_value):
    rows = memory.shape[0]
    whole = lambda array: pl.BlockSpec(array.shape, lambda i: (0, 0))
    return pl.pallas_call(
        pairs_kernel,
        out_shape=(jax.ShapeDtypeStruct((rows, HEAD_DIM), jnp.bfloat16),) * (2 * HEADS),
        grid=(rows // TILE,),
        in_specs=[
            whole(pending_index),
            WHOLE,
            pl.BlockSpec((TILE, DM), lambda i: (i, 0)),
            whole(w_key),
            whole(w_value),
        ],
        out_specs=(pl.BlockSpec((TILE, HEAD_DIM), lambda i: (i, 0)),) * (2 * HEADS),
        compiler_params=pltpu.CompilerParams(
            dimension_semantics=("arbitrary",), vmem_limit_bytes=LARGE
        ),
        cost_estimate=pl.CostEstimate(
            flops=17_200_000_000, bytes_accessed=28_000_000, transcendentals=0
        ),
        name="pairs",
    )(pending_index, pending, memory, w_key, w_value)


SEGMENTS = 16


def attend_kernel(
    queries, key_0, key_1, value_0, value_1, attended, weights, result, numbers, blocks, *rest
):
    pairs, sems = rest[: 2 * HEADS], rest[2 * HEADS]
    capacity = key_0.shape[0] // BR // numbers.shape[0]
    shards = numbers.shape[0]
    segment = capacity * G + META
    batches = shards // SEGMENTS
    loads = [
        pltpu.make_async_copy(there, here, sems.at[1 + number])
        for number, (there, here) in enumerate(zip((key_0, key_1, value_0, value_1), pairs))
    ]
    for copy in loads:
        copy.start()
    for part in range(shards):
        first = part * segment + capacity * G - META * (part % 2)
        notes = queries[first : first + 2 * META, :128].astype(jnp.float32)
        mark = META * (part % 2) + 1
        numbers[part : part + 1, :] = notes[mark : mark + 1, :].astype(jnp.int32)
    copy = pltpu.make_async_copy(numbers, blocks, sems.at[0])
    copy.start()

    keys_wide = SPAN * BR
    rows_high = SPAN * G
    lane = lax.broadcasted_iota(jnp.int32, (rows_high, keys_wide), 1)
    row = lax.broadcasted_iota(jnp.int32, (rows_high, keys_wide), 0)
    own = (lane // BR) == (row // G)
    offset = lax.rem(lax.broadcasted_iota(jnp.int32, (1, keys_wide), 1), BR).astype(jnp.float32)
    groups = capacity // SPAN
    batch_groups = SEGMENTS * groups
    batch_rows = batch_groups * rows_high
    copy.wait()

    def slices(array, step, part, group):
        where = step * SEGMENTS + part
        return jnp.concatenate(
            [
                array[pl.ds(pl.multiple_of(blocks[where, group * SPAN + item] * BR, BR), BR), :]
                for item in range(SPAN)
            ],
            0,
        )

    for head in range(HEADS):
        columns = slice(head * HEAD_DIM, (head + 1) * HEAD_DIM)
        loads[head].wait()

        @pl.loop(0, batches)
        def _(step):
            scores = []
            for part in range(SEGMENTS):
                shift = META * (part % 2)
                top = pl.multiple_of((step * SEGMENTS + part) * segment - shift, 2 * META)
                told = queries[pl.ds(top + capacity * G, 2 * META), :].astype(jnp.float32)
                told = told[shift : shift + 1, :]
                for group in range(groups):
                    length = told[0:1, group * keys_wide : (group + 1) * keys_wide]
                    usable = own & (offset < length)
                    query = queries[pl.ds(top + group * rows_high, rows_high + 2 * shift), columns]
                    if shift:
                        query = query.astype(jnp.float32)[shift : shift + rows_high]
                        query = query.astype(jnp.bfloat16)
                    score = lax.dot_general(
                        query,
                        slices(pairs[head], step, part, group),
                        (((1,), (1,)), ((), ())),
                        preferred_element_type=jnp.float32,
                    ) * (1.0 / 16.0)
                    scores.append(jnp.where(usable, score, MASKED))
            scores = jnp.concatenate(scores, 0)
            expons = jnp.exp(scores - jnp.max(scores, axis=1, keepdims=True))
            first = pl.multiple_of(step * batch_rows, batch_rows)
            weights[head, pl.ds(first, batch_rows), :] = (
                expons * (1.0 / jnp.sum(expons, axis=1, keepdims=True))
            ).astype(jnp.bfloat16)

    for head in range(HEADS):
        columns = slice(head * HEAD_DIM, (head + 1) * HEAD_DIM)
        loads[HEADS + head].wait()

        @pl.loop(0, batches)
        def _(step):
            for part in range(SEGMENTS):
                for group in range(groups):
                    place = step * batch_rows + (part * groups + group) * rows_high
                    rows = pl.ds(pl.multiple_of(place, rows_high), rows_high)
                    result[rows, columns] = jnp.dot(
                        weights[head, rows, :],
                        slices(pairs[HEADS + head], step, part, group),
                        preferred_element_type=jnp.float32,
                    ).astype(jnp.bfloat16)
                if head == HEADS - 1 and part % 2 == 1:
                    high = 2 * groups * rows_high
                    place = step * batch_rows + part // 2 * high
                    done = pl.ds(pl.multiple_of(place, high), high)
                    pltpu.make_async_copy(
                        result.at[done, :], attended.at[done, :], sems.at[0]
                    ).start()

    pltpu.make_async_copy(result, attended, sems.at[0]).wait()


def attend(queries, pairs, shards, nslots):
    return pl.pallas_call(
        attend_kernel,
        out_shape=hbm_out((nslots * G, DM), jnp.bfloat16),
        in_specs=[WHOLE] + [THERE] * (2 * HEADS),
        out_specs=THERE,
        scratch_shapes=[
            pltpu.VMEM((HEADS, nslots * G, SPAN * BR), jnp.bfloat16),
            pltpu.VMEM((nslots * G, DM), jnp.bfloat16),
            pltpu.VMEM((shards, 128), jnp.int32),
            pltpu.SMEM((shards, 128), jnp.int32),
        ]
        + [pltpu.VMEM(array.shape, jnp.bfloat16) for array in pairs]
        + [pltpu.SemaphoreType.DMA((1 + 2 * HEADS,))],
        compiler_params=pltpu.CompilerParams(vmem_limit_bytes=LARGE),
        cost_estimate=pl.CostEstimate(
            flops=4_000_000_000, bytes_accessed=20_000_000, transcendentals=1_000_000
        ),
        name="attend",
    )(queries, *[in_hbm(array) for array in pairs])


def gate_kernel(messages, source, w_input, w_hidden, sums):
    msg = messages.shape[1]
    spoken = jnp.dot(messages[...], w_input[:msg, :], preferred_element_type=jnp.float32)
    hidden = jnp.dot(source[...], w_hidden[...], preferred_element_type=jnp.float32)
    sums[:, : 2 * DM] = spoken[:, : 2 * DM] + hidden[:, : 2 * DM]
    sums[:, 2 * DM : 3 * DM] = spoken[:, 2 * DM :]
    sums[:, 3 * DM :] = hidden[:, 2 * DM :]


def make_gates(messages, source, w_input, w_hidden):
    events, msg = messages.shape
    high = 256
    whole = lambda array: pl.BlockSpec(array.shape, lambda i: (0, 0))
    part = lambda wide: pl.BlockSpec((high, wide), lambda i: (i, 0))
    return pl.pallas_call(
        gate_kernel,
        out_shape=jax.ShapeDtypeStruct((events, 4 * DM), jnp.float32),
        grid=(events // high,),
        in_specs=[part(msg), part(DM), whole(w_input), whole(w_hidden)],
        out_specs=part(4 * DM),
        compiler_params=pltpu.CompilerParams(
            dimension_semantics=("arbitrary",), vmem_limit_bytes=LARGE
        ),
        cost_estimate=pl.CostEstimate(
            flops=2_400_000_000, bytes_accessed=15_000_000, transcendentals=0
        ),
        name="gates",
    )(messages, source, w_input, w_hidden)


LOADED = 256


def update_kernel(
    position,
    returned,
    sums,
    source,
    w_input,
    fresh,
    sums_here,
    source_here,
    weight,
    ordered,
    result,
    sems,
):
    events = source.shape[0]
    base = w_input.shape[0] - weight.shape[0]
    edges = [0, PART, 2 * PART] + list(range(2 * PART + LOADED, events + 1, LOADED))
    loads = {}
    pieces = 0
    for low, top in zip(edges[:-1], edges[1:]):
        rows = slice(low, top)
        loads[low] = [
            pltpu.make_async_copy(there.at[rows, :], here.at[rows, :], sems.at[1 + pieces + kind])
            for kind, (there, here) in enumerate(((sums, sums_here), (source, source_here)))
        ]
        pieces += 2
    first_load = pltpu.make_async_copy(w_input.at[base:, :], weight, sems.at[0])
    first_load.start()
    for low in edges[:-1]:
        for copy in loads[low]:
            copy.start()
    copies = []
    for number in range(events // PART):
        rows = slice(number * PART, (number + 1) * PART)
        for item in range(PART // G):
            place = position[number * (PART // G) + item]
            couple = pl.multiple_of((place // 2) * 2 * G, 2 * G)
            pair = returned[pl.ds(couple, 2 * G), :].astype(jnp.float32)
            top = number * PART + item * G
            ordered[top : top + G, :] = jnp.where(
                lax.rem(place, 2) == 0, pair[:G, :], pair[G:, :]
            )
        if number == 0:
            first_load.wait()
        attended = ordered[rows, :].astype(jnp.bfloat16)
        gates = jnp.dot(attended, weight[...], preferred_element_type=jnp.float32)
        for copy in loads.get(number * PART, []):
            copy.wait()
        reset = jax.nn.sigmoid(gates[:, :DM] + sums_here[rows, :DM])
        update = jax.nn.sigmoid(gates[:, DM : 2 * DM] + sums_here[rows, DM : 2 * DM])
        candidate = jnp.tanh(
            gates[:, 2 * DM :] + sums_here[rows, 2 * DM : 3 * DM] + reset * sums_here[rows, 3 * DM :]
        )
        result[rows, :] = (
            (1.0 - update) * candidate + update * source_here[rows, :].astype(jnp.float32)
        ).astype(jnp.bfloat16)
        copies.append(
            pltpu.make_async_copy(
                result.at[rows, :], fresh.at[rows, :], sems.at[1 + pieces + number]
            )
        )
        copies[-1].start()
    for copy in copies:
        copy.wait()


def updated(position, returned, sums, source, w_input):
    events = source.shape[0]
    return pl.pallas_call(
        update_kernel,
        out_shape=hbm_out((events, DM), jnp.bfloat16),
        in_specs=[SCALARS, WHOLE] + [THERE] * 3,
        out_specs=THERE,
        scratch_shapes=[
            pltpu.VMEM(sums.shape, jnp.float32),
            pltpu.VMEM(source.shape, jnp.bfloat16),
            pltpu.VMEM((DM, 3 * DM), jnp.bfloat16),
            pltpu.VMEM((events, DM), jnp.float32),
            pltpu.VMEM((events, DM), jnp.bfloat16),
            pltpu.SemaphoreType.DMA((3 + 2 * (events // LOADED) + events // PART,)),
        ],
        compiler_params=pltpu.CompilerParams(vmem_limit_bytes=LARGE),
        cost_estimate=pl.CostEstimate(
            flops=1_700_000_000, bytes_accessed=15_000_000, transcendentals=1_500_000
        ),
        name="update",
    )(position, returned, *[in_hbm(array) for array in (sums, source, w_input)])


def body(
    memory,
    sectioned_rows,
    sectioned_index,
    src_local,
    messages,
    block_owner,
    block_local,
    block_len,
    w_query,
    w_key,
    w_value,
    w_input,
    w_hidden,
):
    shards = lax.axis_size("mem")
    nblocks = block_local.shape[0]
    capacity = max(2, 2 * nblocks // shards)
    nslots = shards * capacity

    pending_index = shifted(sectioned_index, "loop", 1)[None, :]
    pending = shifted(sectioned_rows, "loop", 1)

    owners = block_owner[:, 0]
    onehot = (owners[:, None] == jnp.arange(shards, dtype=jnp.int32)[None, :]).astype(jnp.int32)
    rank = jnp.sum((jnp.cumsum(onehot, 0) - onehot) * onehot, 1)
    position = owners * capacity + rank
    unused = (lax.axis_index("mem") * capacity + jnp.arange(nslots, dtype=jnp.int32) % capacity) * 64
    wanted = unused.at[position].set(block_local * 64 + block_len)
    wanted = wanted.reshape(shards, capacity)
    notes = jnp.zeros((shards, META, DM), jnp.int32)
    notes = notes.at[:, 0, : capacity * BR].set(jnp.repeat(wanted % 64, BR, axis=1))
    notes = notes.at[:, 1, :capacity].set(wanted // 64)
    notes = notes.astype(jnp.float32).reshape(shards * META, DM)

    base = memory[src_local]
    prepared = prepare(src_local[:, None], pending_index, base, messages, w_query)
    queries, source = make_queries(position, prepared, notes, pending, nslots)
    segment = capacity * G + META
    arrived = lax.all_to_all(
        queries.reshape(shards, segment, DM), "mem", split_axis=0, concat_axis=0, tiled=True
    )
    pairs = make_pairs(pending_index, pending, memory, w_key, w_value)
    attended = attend(arrived.reshape(shards * segment, DM), pairs, shards, nslots)
    returned = lax.all_to_all(
        attended.reshape(shards, capacity * G, DM), "mem", split_axis=0, concat_axis=0, tiled=True
    ).reshape(nslots * G, DM)

    sums = make_gates(messages, source, w_input, w_hidden)
    return updated(position, returned, sums, source, w_input)


def solution(mesh):
    placed = (
        P("mem", None),
        P(("loop", "mem"), None),
        P(("loop", "mem")),
        P(("loop", "mem")),
        P(("loop", "mem"), None),
        P(("loop", "mem"), None),
        P(("loop", "mem")),
        P(("loop", "mem")),
        P(),
        P(),
        P(),
        P(),
        P(),
    )
    return jax.shard_map(
        body, mesh=mesh, in_specs=placed, out_specs=P(("loop", "mem"), None), check_vma=False
    )
```

```python
import jax
import jax.numpy as jnp
from jax import lax
from jax.experimental import pallas as pl
from jax.experimental.pallas import tpu as pltpu
from jax.sharding import PartitionSpec as P

DM = 512
HEADS = 2
HEAD_DIM = 256
BR = 32
G = 8
SMALL = 24 * 1024 * 1024
LARGE = 48 * 1024 * 1024
SPAN = 8
MASKED = -1e30


def shifted(block, axis, distance):
    size = lax.axis_size(axis)
    route = [((i - distance) % size, i) for i in range(size)]
    return lax.ppermute(block, axis, route)


CHUNK = 512
PART = 128
TILE = 512
META = 8


def vmem_out(shape, dtype):
    return pltpu.VMEM(shape, dtype)


def hbm_out(shape, dtype):
    return pltpu.HBM(shape, dtype)


def in_hbm(array):
    return pltpu.with_memory_space_constraint(array, pltpu.HBM)


WHOLE = pl.BlockSpec(memory_space=pltpu.VMEM)
THERE = pl.BlockSpec(memory_space=pl.ANY)
SCALARS = pl.BlockSpec(memory_space=pltpu.SMEM)


def prepare_kernel(
    source_index, pending_index, base, messages, w_query, chosen, hit, held, spoken, weight
):
    held[...] = base[...]
    weight[...] = w_query[:DM, :]
    for start in range(0, base.shape[0], CHUNK):
        rows = slice(start, start + CHUNK)
        same = jnp.where(source_index[rows, :] == pending_index[...], 1.0, 0.0)
        chosen[rows, :] = same.astype(jnp.bfloat16)
        hit[rows, :] = jnp.broadcast_to(jnp.max(same, axis=1, keepdims=True), (CHUNK, 128))
        spoken[rows, :] = jnp.dot(
            messages[rows, :], w_query[DM:, :], preferred_element_type=jnp.float32
        )


def prepare(source_index, pending_index, base, messages, w_query):
    events = base.shape[0]
    return pl.pallas_call(
        prepare_kernel,
        out_shape=(
            vmem_out((events, pending_index.shape[1]), jnp.bfloat16),
            vmem_out((events, 128), jnp.float32),
            vmem_out((events, DM), jnp.bfloat16),
            vmem_out((events, DM), jnp.float32),
            vmem_out((DM, DM), jnp.bfloat16),
        ),
        in_specs=[WHOLE] * 5,
        out_specs=(WHOLE,) * 5,
        compiler_params=pltpu.CompilerParams(vmem_limit_bytes=SMALL),
        cost_estimate=pl.CostEstimate(
            flops=300_000_000, bytes_accessed=8_000_000, transcendentals=0
        ),
        name="prepare",
    )(source_index, pending_index, base, messages, w_query)


def query_kernel(
    position,
    chosen,
    hit,
    base,
    spoken,
    w_query,
    notes,
    pending,
    slots,
    source,
    staged,
    packed,
    kept,
    sems,
):
    events = base.shape[0]
    owners = notes.shape[0] // META
    high = staged.shape[0] // owners
    segment = high + META
    copies = []
    for start in range(0, events, CHUNK):
        rows = slice(start, start + CHUNK)
        picked = jnp.dot(chosen[rows, :], pending[...], preferred_element_type=jnp.float32)
        merged = jnp.where(
            hit[rows, :1] > 0.0, picked, base[rows, :].astype(jnp.float32)
        ).astype(jnp.bfloat16)
        kept[rows, :] = merged
        found = jnp.dot(merged, w_query[...], preferred_element_type=jnp.float32) + spoken[rows, :]
        for item in range(CHUNK // G):
            place = pl.multiple_of(position[start // G + item] * G, G)
            staged[pl.ds(place, G), :] = found[item * G : (item + 1) * G, :]
        copies.append(
            pltpu.make_async_copy(kept.at[rows, :], source.at[rows, :], sems.at[start // CHUNK])
        )
        copies[-1].start()
    others = len(copies)
    parts = 8
    for part in range(parts):
        for owner in range(part * owners // parts, (part + 1) * owners // parts, 2):
            couple = [
                piece
                for each in (owner, owner + 1)
                for piece in (
                    staged[each * high : (each + 1) * high, :],
                    notes[each * META : (each + 1) * META, :],
                )
            ]
            packed[owner * segment : (owner + 2) * segment, :] = jnp.concatenate(couple, 0).astype(
                jnp.bfloat16
            )
        span = owners // parts * segment
        rows = slice(part * span, (part + 1) * span)
        copies.append(
            pltpu.make_async_copy(packed.at[rows, :], slots.at[rows, :], sems.at[others + part])
        )
        copies[-1].start()
    for copy in copies:
        copy.wait()


def make_queries(position, prepared, notes, pending, nslots):
    events = pending.shape[0]
    total = nslots * G + notes.shape[0]
    return pl.pallas_call(
        query_kernel,
        out_shape=(hbm_out((total, DM), jnp.bfloat16), hbm_out((events, DM), jnp.bfloat16)),
        in_specs=[SCALARS] + [WHOLE] * 7,
        out_specs=(THERE, THERE),
        scratch_shapes=[
            pltpu.VMEM((nslots * G, DM), jnp.float32),
            pltpu.VMEM((total, DM), jnp.bfloat16),
            pltpu.VMEM((events, DM), jnp.bfloat16),
            pltpu.SemaphoreType.DMA((8 + events // CHUNK,)),
        ],
        compiler_params=pltpu.CompilerParams(vmem_limit_bytes=SMALL),
        cost_estimate=pl.CostEstimate(
            flops=2_000_000_000, bytes_accessed=8_000_000, transcendentals=0
        ),
        name="queries",
    )(position, *prepared, notes, pending)


def pairs_kernel(pending_index, pending, memory, w_key, w_value, *pairs):
    first = pl.program_id(0) * TILE
    row = first + lax.broadcasted_iota(jnp.int32, (TILE, 1), 0)
    chosen = jnp.where(row == pending_index[...], 1.0, 0.0)
    hit = jnp.max(chosen, axis=1, keepdims=True) > 0.0
    picked = jnp.dot(chosen.astype(jnp.bfloat16), pending[...], preferred_element_type=jnp.float32)
    merged = jnp.where(hit, picked, memory[...].astype(jnp.float32)).astype(jnp.bfloat16)
    for weight, part in ((w_key, pairs[:HEADS]), (w_value, pairs[HEADS:])):
        rows = jnp.dot(merged, weight[...], preferred_element_type=jnp.float32).astype(jnp.bfloat16)
        for head in range(HEADS):
            part[head][...] = rows[:, head * HEAD_DIM : (head + 1) * HEAD_DIM]


def make_pairs(pending_index, pending, memory, w_key, w_value):
    rows = memory.shape[0]
    whole = lambda array: pl.BlockSpec(array.shape, lambda i: (0, 0))
    return pl.pallas_call(
        pairs_kernel,
        out_shape=(jax.ShapeDtypeStruct((rows, HEAD_DIM), jnp.bfloat16),) * (2 * HEADS),
        grid=(rows // TILE,),
        in_specs=[
            whole(pending_index),
            WHOLE,
            pl.BlockSpec((TILE, DM), lambda i: (i, 0)),
            whole(w_key),
            whole(w_value),
        ],
        out_specs=(pl.BlockSpec((TILE, HEAD_DIM), lambda i: (i, 0)),) * (2 * HEADS),
        compiler_params=pltpu.CompilerParams(
            dimension_semantics=("arbitrary",), vmem_limit_bytes=LARGE
        ),
        cost_estimate=pl.CostEstimate(
            flops=17_200_000_000, bytes_accessed=28_000_000, transcendentals=0
        ),
        name="pairs",
    )(pending_index, pending, memory, w_key, w_value)


SEGMENTS = 16


def attend_kernel(
    queries, key_0, key_1, value_0, value_1, attended, weights, result, numbers, blocks, *rest
):
    pairs, sems = rest[: 2 * HEADS], rest[2 * HEADS]
    capacity = key_0.shape[0] // BR // numbers.shape[0]
    shards = numbers.shape[0]
    segment = capacity * G + META
    batches = shards // SEGMENTS
    loads = [
        pltpu.make_async_copy(there, here, sems.at[1 + number])
        for number, (there, here) in enumerate(zip((key_0, key_1, value_0, value_1), pairs))
    ]
    high = key_0.shape[0] // 4
    for number, (there, here) in enumerate(zip((key_0, key_1, value_0, value_1), pairs)):
        for low in range(0, key_0.shape[0], high):
            pltpu.make_async_copy(
                there.at[low : low + high, :], here.at[low : low + high, :], sems.at[1 + number]
            ).start()
    for part in range(shards):
        first = part * segment + capacity * G - META * (part % 2)
        notes = queries[first : first + 2 * META, :128].astype(jnp.float32)
        mark = META * (part % 2) + 1
        numbers[part : part + 1, :] = notes[mark : mark + 1, :].astype(jnp.int32)
    copy = pltpu.make_async_copy(numbers, blocks, sems.at[0])
    copy.start()

    keys_wide = SPAN * BR
    rows_high = SPAN * G
    lane = lax.broadcasted_iota(jnp.int32, (rows_high, keys_wide), 1)
    row = lax.broadcasted_iota(jnp.int32, (rows_high, keys_wide), 0)
    own = (lane // BR) == (row // G)
    offset = lax.rem(lax.broadcasted_iota(jnp.int32, (1, keys_wide), 1), BR).astype(jnp.float32)
    groups = capacity // SPAN
    batch_groups = SEGMENTS * groups
    batch_rows = batch_groups * rows_high
    copy.wait()

    def slices(array, step, part, group):
        where = step * SEGMENTS + part
        return jnp.concatenate(
            [
                array[pl.ds(pl.multiple_of(blocks[where, group * SPAN + item] * BR, BR), BR), :]
                for item in range(SPAN)
            ],
            0,
        )

    for head in range(HEADS):
        columns = slice(head * HEAD_DIM, (head + 1) * HEAD_DIM)
        loads[head].wait()

        @pl.loop(0, batches)
        def _(step):
            scores = []
            for part in range(SEGMENTS):
                shift = META * (part % 2)
                top = pl.multiple_of((step * SEGMENTS + part) * segment - shift, 2 * META)
                told = queries[pl.ds(top + capacity * G, 2 * META), :].astype(jnp.float32)
                told = told[shift : shift + 1, :]
                for group in range(groups):
                    length = told[0:1, group * keys_wide : (group + 1) * keys_wide]
                    usable = own & (offset < length)
                    query = queries[pl.ds(top + group * rows_high, rows_high + 2 * shift), columns]
                    if shift:
                        query = query.astype(jnp.float32)[shift : shift + rows_high]
                        query = query.astype(jnp.bfloat16)
                    score = lax.dot_general(
                        query,
                        slices(pairs[head], step, part, group),
                        (((1,), (1,)), ((), ())),
                        preferred_element_type=jnp.float32,
                    ) * (1.0 / 16.0)
                    scores.append(jnp.where(usable, score, MASKED))
            scores = jnp.concatenate(scores, 0)
            expons = jnp.exp(scores - jnp.max(scores, axis=1, keepdims=True))
            first = pl.multiple_of(step * batch_rows, batch_rows)
            weights[head, pl.ds(first, batch_rows), :] = (
                expons * (1.0 / jnp.sum(expons, axis=1, keepdims=True))
            ).astype(jnp.bfloat16)

    for head in range(HEADS):
        columns = slice(head * HEAD_DIM, (head + 1) * HEAD_DIM)
        loads[HEADS + head].wait()

        @pl.loop(0, batches)
        def _(step):
            for part in range(SEGMENTS):
                for group in range(groups):
                    place = step * batch_rows + (part * groups + group) * rows_high
                    rows = pl.ds(pl.multiple_of(place, rows_high), rows_high)
                    result[rows, columns] = jnp.dot(
                        weights[head, rows, :],
                        slices(pairs[HEADS + head], step, part, group),
                        preferred_element_type=jnp.float32,
                    ).astype(jnp.bfloat16)
                if head == HEADS - 1 and part % 2 == 1:
                    high = 2 * groups * rows_high
                    place = step * batch_rows + part // 2 * high
                    done = pl.ds(pl.multiple_of(place, high), high)
                    pltpu.make_async_copy(
                        result.at[done, :], attended.at[done, :], sems.at[0]
                    ).start()

    pltpu.make_async_copy(result, attended, sems.at[0]).wait()


def attend(queries, pairs, shards, nslots):
    return pl.pallas_call(
        attend_kernel,
        out_shape=hbm_out((nslots * G, DM), jnp.bfloat16),
        in_specs=[WHOLE] + [THERE] * (2 * HEADS),
        out_specs=THERE,
        scratch_shapes=[
            pltpu.VMEM((HEADS, nslots * G, SPAN * BR), jnp.bfloat16),
            pltpu.VMEM((nslots * G, DM), jnp.bfloat16),
            pltpu.VMEM((shards, 128), jnp.int32),
            pltpu.SMEM((shards, 128), jnp.int32),
        ]
        + [pltpu.VMEM(array.shape, jnp.bfloat16) for array in pairs]
        + [pltpu.SemaphoreType.DMA((1 + 2 * HEADS,))],
        compiler_params=pltpu.CompilerParams(vmem_limit_bytes=LARGE),
        cost_estimate=pl.CostEstimate(
            flops=4_000_000_000, bytes_accessed=20_000_000, transcendentals=1_000_000
        ),
        name="attend",
    )(queries, *[in_hbm(array) for array in pairs])


def gate_kernel(messages, source, w_input, w_hidden, sums):
    msg = messages.shape[1]
    spoken = jnp.dot(messages[...], w_input[:msg, :], preferred_element_type=jnp.float32)
    hidden = jnp.dot(source[...], w_hidden[...], preferred_element_type=jnp.float32)
    sums[:, : 2 * DM] = spoken[:, : 2 * DM] + hidden[:, : 2 * DM]
    sums[:, 2 * DM : 3 * DM] = spoken[:, 2 * DM :]
    sums[:, 3 * DM :] = hidden[:, 2 * DM :]


def make_gates(messages, source, w_input, w_hidden):
    events, msg = messages.shape
    high = 256
    whole = lambda array: pl.BlockSpec(array.shape, lambda i: (0, 0))
    part = lambda wide: pl.BlockSpec((high, wide), lambda i: (i, 0))
    return pl.pallas_call(
        gate_kernel,
        out_shape=jax.ShapeDtypeStruct((events, 4 * DM), jnp.float32),
        grid=(events // high,),
        in_specs=[part(msg), part(DM), whole(w_input), whole(w_hidden)],
        out_specs=part(4 * DM),
        compiler_params=pltpu.CompilerParams(
            dimension_semantics=("arbitrary",), vmem_limit_bytes=LARGE
        ),
        cost_estimate=pl.CostEstimate(
            flops=2_400_000_000, bytes_accessed=15_000_000, transcendentals=0
        ),
        name="gates",
    )(messages, source, w_input, w_hidden)


LOADED = 256


def update_kernel(
    position,
    returned,
    sums,
    source,
    w_input,
    fresh,
    sums_here,
    source_here,
    weight,
    ordered,
    result,
    sems,
):
    events = source.shape[0]
    base = w_input.shape[0] - weight.shape[0]
    edges = [0, PART, 2 * PART] + list(range(2 * PART + LOADED, events + 1, LOADED))
    loads = {}
    pieces = 0
    for low, top in zip(edges[:-1], edges[1:]):
        rows = slice(low, top)
        loads[low] = [
            pltpu.make_async_copy(there.at[rows, :], here.at[rows, :], sems.at[1 + pieces + kind])
            for kind, (there, here) in enumerate(((sums, sums_here), (source, source_here)))
        ]
        pieces += 2
    first_load = pltpu.make_async_copy(w_input.at[base:, :], weight, sems.at[0])
    high = weight.shape[0] // 4
    for low in range(0, weight.shape[0], high):
        pltpu.make_async_copy(
            w_input.at[base + low : base + low + high, :], weight.at[low : low + high, :], sems.at[0]
        ).start()
    for low in edges[:-1]:
        for copy in loads[low]:
            copy.start()
    copies = []
    for number in range(events // PART):
        rows = slice(number * PART, (number + 1) * PART)
        for item in range(PART // G):
            place = position[number * (PART // G) + item]
            couple = pl.multiple_of((place // 2) * 2 * G, 2 * G)
            pair = returned[pl.ds(couple, 2 * G), :].astype(jnp.float32)
            top = number * PART + item * G
            ordered[top : top + G, :] = jnp.where(
                lax.rem(place, 2) == 0, pair[:G, :], pair[G:, :]
            )
        if number == 0:
            first_load.wait()
        attended = ordered[rows, :].astype(jnp.bfloat16)
        gates = jnp.dot(attended, weight[...], preferred_element_type=jnp.float32)
        for copy in loads.get(number * PART, []):
            copy.wait()
        reset = jax.nn.sigmoid(gates[:, :DM] + sums_here[rows, :DM])
        update = jax.nn.sigmoid(gates[:, DM : 2 * DM] + sums_here[rows, DM : 2 * DM])
        candidate = jnp.tanh(
            gates[:, 2 * DM :] + sums_here[rows, 2 * DM : 3 * DM] + reset * sums_here[rows, 3 * DM :]
        )
        result[rows, :] = (
            (1.0 - update) * candidate + update * source_here[rows, :].astype(jnp.float32)
        ).astype(jnp.bfloat16)
        copies.append(
            pltpu.make_async_copy(
                result.at[rows, :], fresh.at[rows, :], sems.at[1 + pieces + number]
            )
        )
        copies[-1].start()
    for copy in copies:
        copy.wait()


def updated(position, returned, sums, source, w_input):
    events = source.shape[0]
    return pl.pallas_call(
        update_kernel,
        out_shape=hbm_out((events, DM), jnp.bfloat16),
        in_specs=[SCALARS, WHOLE] + [THERE] * 3,
        out_specs=THERE,
        scratch_shapes=[
            pltpu.VMEM(sums.shape, jnp.float32),
            pltpu.VMEM(source.shape, jnp.bfloat16),
            pltpu.VMEM((DM, 3 * DM), jnp.bfloat16),
            pltpu.VMEM((events, DM), jnp.float32),
            pltpu.VMEM((events, DM), jnp.bfloat16),
            pltpu.SemaphoreType.DMA((3 + 2 * (events // LOADED) + events // PART,)),
        ],
        compiler_params=pltpu.CompilerParams(vmem_limit_bytes=LARGE),
        cost_estimate=pl.CostEstimate(
            flops=1_700_000_000, bytes_accessed=15_000_000, transcendentals=1_500_000
        ),
        name="update",
    )(position, returned, *[in_hbm(array) for array in (sums, source, w_input)])


def body(
    memory,
    sectioned_rows,
    sectioned_index,
    src_local,
    messages,
    block_owner,
    block_local,
    block_len,
    w_query,
    w_key,
    w_value,
    w_input,
    w_hidden,
):
    shards = lax.axis_size("mem")
    nblocks = block_local.shape[0]
    capacity = max(2, 2 * nblocks // shards)
    nslots = shards * capacity

    pending_index = shifted(sectioned_index, "loop", 1)[None, :]
    pending = shifted(sectioned_rows, "loop", 1)

    owners = block_owner[:, 0]
    onehot = (owners[:, None] == jnp.arange(shards, dtype=jnp.int32)[None, :]).astype(jnp.int32)
    rank = jnp.sum((jnp.cumsum(onehot, 0) - onehot) * onehot, 1)
    position = owners * capacity + rank
    unused = (lax.axis_index("mem") * capacity + jnp.arange(nslots, dtype=jnp.int32) % capacity) * 64
    wanted = unused.at[position].set(block_local * 64 + block_len)
    wanted = wanted.reshape(shards, capacity)
    notes = jnp.zeros((shards, META, DM), jnp.int32)
    notes = notes.at[:, 0, : capacity * BR].set(jnp.repeat(wanted % 64, BR, axis=1))
    notes = notes.at[:, 1, :capacity].set(wanted // 64)
    notes = notes.astype(jnp.float32).reshape(shards * META, DM)

    base = memory[src_local]
    prepared = prepare(src_local[:, None], pending_index, base, messages, w_query)
    queries, source = make_queries(position, prepared, notes, pending, nslots)
    segment = capacity * G + META
    arrived = lax.all_to_all(
        queries.reshape(shards, segment, DM), "mem", split_axis=0, concat_axis=0, tiled=True
    )
    pairs = make_pairs(pending_index, pending, memory, w_key, w_value)
    attended = attend(arrived.reshape(shards * segment, DM), pairs, shards, nslots)
    returned = lax.all_to_all(
        attended.reshape(shards, capacity * G, DM), "mem", split_axis=0, concat_axis=0, tiled=True
    ).reshape(nslots * G, DM)

    sums = make_gates(messages, source, w_input, w_hidden)
    return updated(position, returned, sums, source, w_input)


def solution(mesh):
    placed = (
        P("mem", None),
        P(("loop", "mem"), None),
        P(("loop", "mem")),
        P(("loop", "mem")),
        P(("loop", "mem"), None),
        P(("loop", "mem"), None),
        P(("loop", "mem")),
        P(("loop", "mem")),
        P(),
        P(),
        P(),
        P(),
        P(),
    )
    return jax.shard_map(
        body, mesh=mesh, in_specs=placed, out_specs=P(("loop", "mem"), None), check_vma=False
    )
```
